256 devices in a mesh: rep: 2 (over core), section: 4 (over y), exp: 32 (over z, x).
Axes of the slice: x: 4, y: 4, z: 8, core: 2. Of those that a mesh axis runs over, the one named last changes fastest.
Arguments:
- row_codes: bfloat16 [4, 4096, 2048], P('section', ('rep', 'exp')), may hold values from -448 to 448
- block_exponents: int32 [4, 4096, 16], P('section', ('rep', 'exp')), may hold values from -10 to -6
- routes: int32 [4, 4096, 8], P('section', ('rep', 'exp')), may hold values from 0 to 63, all different within a row; in each aligned block of 64 rows (0 to 63, 64 to 127, ..., all dimensions but the last counted through in order) at most 12 rows name the same one
- route_weight: float32 [4, 4096, 8], P('section', ('rep', 'exp')), may hold values from 0.02 to 0.3
- out_grad: bfloat16 [4, 4096, 2048], P('section', ('rep', 'exp')), may hold values from -6 to 6
- gate_weight: bfloat16 [4, 64, 384, 2048], P('section', 'exp', 'rep'), may hold values from -0.125 to 0.125
- up_weight: bfloat16 [4, 64, 384, 2048], P('section', 'exp', 'rep'), may hold values from -0.125 to 0.125
- down_weight: bfloat16 [4, 64, 384, 2048], P('section', 'exp', 'rep'), may hold values from -0.3125 to 0.3125
Outputs:
- next_rows: bfloat16 [4, 4096, 2048], P('section', ('rep', 'exp'))
- prev_grads: bfloat16 [4, 4096, 2048], P('section', ('rep', 'exp'))
- gate_weight_grad: bfloat16 [4, 64, 384, 2048], P('section', 'exp', 'rep')
- up_weight_grad: bfloat16 [4, 64, 384, 2048], P('section', 'exp', 'rep')
- down_weight_grad: bfloat16 [4, 64, 384, 2048], P('section', 'exp', 'rep')
The draws below stay inside these ranges and needn't reach their ends.
Inputs may be any that keep to these rules, and one draw needn't show every extreme that they name: `routes`: the 8 experts of a token differ. In the 64 rows of one device of a layer no expert is named by more than 12 rows, a bound that some of them reach.
All inputs are finite; a program needn't handle non-finite values.
Results may differ from the reference program's by a relative error of at most 0.0065.
Values may be sent and summed in bfloat16 or wider, within the bound.
A program may use at most 128 MiB of HBM per device.

```python
import math
import jax
import jax.numpy as jnp
import numpy as np
from jax import lax

D = 2048
FF = 384
TOPK = 8
TOK_DEV = 64
SECTIONS = 4
EXPERTS = 64
TOKENS = 4096
NB = 16
CAP = 12
N_REP = 2
N_EXP = 32


def set_ends(result, key, least, top_value):
    longest = result.shape.index(max(result.shape))
    spots = []
    for shift in (0, 1):
        where = [jax.random.randint(jax.random.fold_in(key, axis), (), 0, length) for axis, length in enumerate(result.shape)]
        where[longest] = (where[longest] + shift) % result.shape[longest]
        spots.append(tuple(where))
    return result.at[spots[0]].set(least).at[spots[1]].set(top_value)


def level_of(key, extent, shards, smallest, top_value):
    factor_of, own = 1.0, jax.random.fold_in(key, 6)
    for position, blocks in shards:
        steps = jnp.exp(jax.random.uniform(jax.random.fold_in(own, position), (blocks,), jnp.float32, smallest / len(shards), top_value / len(shards)))
        factor_of = factor_of * jnp.repeat(steps, extent[position] // blocks).reshape([-1 if axis == position else 1 for axis in range(len(extent))])
    return factor_of


def routed_block(own_key, own, number, rows, amount, top, most, slope):
    ranking = jax.random.permutation(own_key, amount)
    packed, ordinary = shares(amount, rows * top, most, slope, True), shares(amount, rows * top, most, slope, False)
    places = jnp.arange(amount)

    def named(lengths, offset_by):
        used = int((lengths > 0).sum())
        fixed = max(1, used // 4)
        moved = fixed + (places - fixed + offset_by * (used - fixed)) % max(1, amount - fixed)
        return jnp.zeros((amount,), jnp.int32).at[ranking[jnp.where(places < fixed, places, moved)]].set(jnp.asarray(lengths, jnp.int32))

    lengths = jnp.where(number % 4 == 0, named(packed, number // 4), named(ordinary, number - number // 4 - 1))
    mixed = jax.random.permutation(jax.random.fold_in(own, 3), amount)
    giver, sink = mixed[0:amount // 2 * 2:2], mixed[1:amount // 2 * 2:2]
    room = jnp.minimum(lengths[giver] - 1, most - lengths[sink]) // 2
    room = jnp.where((giver == ranking[0]) | (sink == ranking[0]) | (lengths[sink] == 0), 0, jnp.maximum(room, 0))
    moved = jax.random.randint(jax.random.fold_in(own, 4), (amount // 2,), 0, 1 << 20) % (room + 1)
    lengths = lengths.at[giver].add(-moved).at[sink].add(moved)
    labels = jnp.searchsorted(jnp.cumsum(lengths), jnp.arange(rows * top), side="right").astype(jnp.int32)
    table = labels.reshape(top, rows).T
    table = table[jax.random.permutation(jax.random.fold_in(own, 1), rows)]
    offset_by = jax.random.randint(jax.random.fold_in(own, 2), (rows, 1), 0, top)
    return jnp.take_along_axis(table, (jnp.arange(top)[None, :] + offset_by) % top, axis=1)


def shares(amount, total, most, skew, full):
    portions = [(1 << 20) // math.isqrt(grade ** skew) + 1 for grade in range(1, amount + 1)]
    largest = most if full else min(most, max(-(-total // amount), total * portions[0] // sum(portions)))
    least = 1 if total - largest >= amount - 1 else 0
    given, surplus = [largest] + [least] * (amount - 1), total - largest - least * (amount - 1)
    while surplus > 0:
        movable = [i for i in range(1, amount) if given[i] < largest] or [i for i in range(1, amount) if given[i] < most]
        mass, budget = sum([portions[i] for i in movable]), surplus
        for i in movable:
            more = min(most - given[i], max(1, budget * portions[i] // mass), surplus)
            given[i] = given[i] + more
            surplus = surplus - more
    return np.array(given)


def noise(stream_key, extent, spread, most, cuts=(), kind=jnp.bfloat16):
    array = jax.random.normal(stream_key, extent, jnp.float32) * spread
    if len(cuts) > 0:
        array = level_of(stream_key, extent, cuts, -0.22, 0.18) * array
    return jnp.clip(array, min=-most, max=most).astype(kind)


def setup_inputs(seed: int = 0) -> dict:
    arg_keys = jax.random.split(jax.random.key(seed), 9)
    row_codes = noise(arg_keys[0], (SECTIONS, TOKENS, D), 96.0, 448.0, ((0, 4), (1, 64)))
    block_exponents = set_ends(jax.random.randint(arg_keys[1], (SECTIONS, TOKENS, NB), -10, -5), jax.random.fold_in(arg_keys[1], 1), -10, (-5) - 1).astype(jnp.int32)
    routes_keys = jax.random.split(jax.random.fold_in(arg_keys[2], 1), SECTIONS * TOKENS // TOK_DEV)
    routes_turns = jax.random.permutation(jax.random.fold_in(arg_keys[2], 3), SECTIONS * TOKENS // TOK_DEV)
    routes = jax.vmap(lambda own, number: routed_block(jax.random.fold_in(arg_keys[2], 2), own, number, TOK_DEV, EXPERTS, TOPK, CAP, 2))(routes_keys, routes_turns).reshape((SECTIONS, TOKENS, TOPK))
    route_weight = jnp.clip(jnp.exp(math.log(0.3) - 2.7080503 * jax.random.uniform(arg_keys[3], (SECTIONS, TOKENS, TOPK), jnp.float32) ** level_of(arg_keys[3], (SECTIONS, TOKENS, TOPK), ((0, 4), (1, 64)), -0.2, 0.2)), 0.02, 0.3)
    out_grad = noise(arg_keys[4], (SECTIONS, TOKENS, D), 1.0, 6.0, ((0, 4), (1, 64)))
    gate_weight = noise(arg_keys[5], (SECTIONS, EXPERTS, FF, D), D ** -0.5, 0.125, ((0, 4), (1, 32), (2, 2)))
    up_weight = noise(arg_keys[6], (SECTIONS, EXPERTS, FF, D), D ** -0.5, 0.125, ((0, 4), (1, 32), (2, 2)))
    down_weight = noise(arg_keys[7], (SECTIONS, EXPERTS, FF, D), FF ** -0.5, 0.3125, ((0, 4), (1, 32), (2, 2)))
    return {"row_codes": row_codes, "block_exponents": block_exponents, "routes": routes, "route_weight": route_weight, "out_grad": out_grad, "gate_weight": gate_weight, "up_weight": up_weight, "down_weight": down_weight}


def dequantize(code_rows, exponent_rows):
    row_count = code_rows.shape[0]
    row_width = code_rows.shape[1]
    blocks = code_rows.astype(jnp.float32).reshape(row_count, row_width // 128, 128)
    scales = jnp.exp2(exponent_rows.astype(jnp.float32))[:, :, None]
    return (blocks * scales).reshape(row_count, row_width).astype(jnp.bfloat16)


def expert_pass(expert_rows, gated_grad, gate_rows, up_rows, down_rows):
    gate_act = jnp.dot(expert_rows, gate_rows.T, preferred_element_type=jnp.float32)
    up_act = jnp.dot(expert_rows, up_rows.T, preferred_element_type=jnp.float32)
    sigmoid_gate = jax.nn.sigmoid(gate_act)
    swish = gate_act * sigmoid_gate
    hidden = (swish * up_act).astype(jnp.bfloat16)
    output = jnp.dot(hidden, down_rows, preferred_element_type=jnp.float32).astype(jnp.bfloat16)
    hidden_grad = jnp.dot(gated_grad, down_rows.T, preferred_element_type=jnp.float32)
    gate_grad = (hidden_grad * up_act * sigmoid_gate * (1.0 + gate_act * (1.0 - sigmoid_gate))).astype(jnp.bfloat16)
    up_grad = (hidden_grad * swish).astype(jnp.bfloat16)
    input_grad = (jnp.dot(gate_grad, gate_rows, preferred_element_type=jnp.float32)
                  + jnp.dot(up_grad, up_rows, preferred_element_type=jnp.float32)).astype(jnp.bfloat16)
    gate_total = jnp.dot(gate_grad.T, expert_rows, preferred_element_type=jnp.float32)
    up_total = jnp.dot(up_grad.T, expert_rows, preferred_element_type=jnp.float32)
    down_total = jnp.dot(hidden.T, gated_grad, preferred_element_type=jnp.float32)
    return output, input_grad, gate_total, up_total, down_total


def replica_layer(section_index, first_row, replica_tokens, row_codes, block_exponents, routes,
                  route_weight, out_grad, gate_weight, up_weight, down_weight):
    assigns = replica_tokens * TOPK
    most_rows = N_EXP * CAP
    last_row = first_row + replica_tokens
    inputs = dequantize(row_codes[section_index, first_row:last_row], block_exponents[section_index, first_row:last_row])
    flat_ids = routes[section_index, first_row:last_row].reshape(-1)
    weights_here = route_weight[section_index, first_row:last_row]
    grad_here = out_grad[section_index, first_row:last_row]
    gated_all = (weights_here[:, :, None] * grad_here[:, None, :].astype(jnp.float32)).astype(jnp.bfloat16)
    gated_all = gated_all.reshape(assigns, D)
    zero_value = jnp.zeros((), jnp.bfloat16)

    def one_expert(expert_id):
        positions = jnp.nonzero(flat_ids == expert_id, size=most_rows, fill_value=assigns)[0].astype(jnp.int32)
        present = positions < assigns
        clipped = jnp.minimum(positions, assigns - 1)
        expert_rows = jnp.where(present[:, None], inputs[clipped // TOPK], zero_value)
        gated_grad = jnp.where(present[:, None], gated_all[clipped], zero_value)
        results = expert_pass(expert_rows, gated_grad, gate_weight[section_index, expert_id],
                              up_weight[section_index, expert_id], down_weight[section_index, expert_id])
        return (positions, results[0], results[1], results[2].astype(jnp.bfloat16),
                results[3].astype(jnp.bfloat16), results[4].astype(jnp.bfloat16))

    mapped = lax.map(one_expert, jnp.arange(EXPERTS, dtype=jnp.int32))
    positions = mapped[0].reshape(-1)
    expert_out = jnp.zeros((assigns + 1, D), jnp.float32).at[positions].set(
        mapped[1].reshape(-1, D).astype(jnp.float32))[:assigns]
    expert_back = jnp.zeros((assigns + 1, D), jnp.float32).at[positions].set(
        mapped[2].reshape(-1, D).astype(jnp.float32))[:assigns]
    layer_out = (inputs.astype(jnp.float32)
                 + jnp.sum(weights_here[:, :, None] * expert_out.reshape(replica_tokens, TOPK, D), axis=1)).astype(jnp.bfloat16)
    layer_back = (grad_here.astype(jnp.float32)
                  + jnp.sum(expert_back.reshape(replica_tokens, TOPK, D), axis=1)).astype(jnp.bfloat16)
    return layer_out, layer_back, mapped[3], mapped[4], mapped[5]


def reference(row_codes, block_exponents, routes, route_weight, out_grad, gate_weight, up_weight, down_weight):
    replica_tokens = TOKENS // N_REP
    forward_list = []
    backward_list = []
    gate_list = []
    up_list = []
    down_list = []
    for section_index in range(SECTIONS):
        out_parts = []
        back_parts = []
        gate_sum = jnp.zeros((EXPERTS, FF, D), jnp.float32)
        up_sum = jnp.zeros((EXPERTS, FF, D), jnp.float32)
        down_sum = jnp.zeros((EXPERTS, FF, D), jnp.float32)
        for replica in range(N_REP):
            results = replica_layer(section_index, replica * replica_tokens, replica_tokens, row_codes,
                                    block_exponents, routes, route_weight, out_grad, gate_weight,
                                    up_weight, down_weight)
            out_parts.append(results[0])
            back_parts.append(results[1])
            gate_sum = gate_sum + results[2].astype(jnp.float32)
            up_sum = up_sum + results[3].astype(jnp.float32)
            down_sum = down_sum + results[4].astype(jnp.float32)
        forward_list.append(jnp.concatenate(out_parts, axis=0))
        backward_list.append(jnp.concatenate(back_parts, axis=0))
        gate_list.append(gate_sum.astype(jnp.bfloat16))
        up_list.append(up_sum.astype(jnp.bfloat16))
        down_list.append(down_sum.astype(jnp.bfloat16))
    next_rows = jnp.roll(jnp.stack(forward_list), 1, axis=0)
    prev_grads = jnp.roll(jnp.stack(backward_list), -1, axis=0)
    return (next_rows, prev_grads, jnp.stack(gate_list), jnp.stack(up_list), jnp.stack(down_list))
```

```python
import functools

import jax
import jax.numpy as jnp
from jax import lax
from jax.experimental import pallas as pl
from jax.experimental.pallas import tpu as pltpu
from jax.sharding import PartitionSpec as P

MESH = pl.DeviceIdType.MESH
NX = 4
NZ = 8
CAP = 12
ORDER = (0, 1, 7, 2, 6, 3, 5, 4)
PLACE = tuple(ORDER.index(slot) for slot in range(NZ))
TILE = 512
F32 = jnp.float32
BF16 = jnp.bfloat16


def dot_nn(a, b):
    return lax.dot_general(a, b, (((1,), (0,)), ((), ())), preferred_element_type=F32)


def dot_nt(a, b):
    return lax.dot_general(a, b, (((1,), (1,)), ((), ())), preferred_element_type=F32)


def kernel(
    codes_ref, exps_ref, routes_ref, rweight_ref, grad_ref, gate_ref, up_ref, down_ref,
    next_ref, prev_ref, gate_out, up_out, down_out,
    zrows, sendrows, arrived, weights, results, returned, reduced, partial, wrecv, final,
    act, hidden, hidden_t, grads, grads_t, meta_src, meta, pick, pick_t, pick_hi, pick_lo, slot_w,
    ring_s, ring_r, meta_s, meta_r, wt_l, wt_s, wt_r, disp_s, disp_r, ret_s, ret_r,
    red_s, red_r, hop_s, hop_r, wg_s, wg_r, out_l,
):
    tokens, width = codes_ref.shape
    unit = sendrows.shape[1]
    half_rows = tokens // 2
    rows = NX * 2 * unit
    half = gate_ref.shape[1]
    full = 2 * half
    tiles = width // TILE
    rep, sec, ex = lax.axis_index("rep"), lax.axis_index("section"), lax.axis_index("exp")
    sections = lax.axis_size("section")
    z, x = lax.div(ex, NX), lax.rem(ex, NX)

    def at_z(k):
        return (rep, sec, lax.rem(z + k, NZ) * NX + x)

    def at_x(k):
        return (rep, sec, z * NX + lax.rem(x + k, NX))

    other_core = (1 - rep, sec, ex)
    sec_next = (rep, lax.rem(sec + 1, sections), ex)
    sec_prev = (rep, lax.rem(sec + sections - 1, sections), ex)

    def remote(src, dst, send, recv, device):
        copy = pltpu.make_async_remote_copy(
            src_ref=src, dst_ref=dst, send_sem=send, recv_sem=recv,
            device_id=device, device_id_type=MESH)
        return copy

    def cols_of(n, size=TILE):
        return pl.ds(pl.multiple_of(n * size, size), size)

    weight_refs = (gate_ref, up_ref, down_ref)
    own_copies = []
    for m in range(3):
        copy = pltpu.make_async_copy(
            weight_refs[m], weights.at[:, pl.ds(m * full, half)], wt_l.at[m])
        copy.start()
        own_copies.append(copy)
    partners = [at_z(k) for k in range(1, NZ)] + [at_x(k) for k in range(1, NX)]
    partners += [other_core, sec_next, sec_prev]
    barrier = pltpu.get_barrier_semaphore()
    for device in partners:
        pl.semaphore_signal(barrier, inc=1, device_id=device, device_id_type=MESH)

    for b in range(width // 128):
        cols = pl.ds(b * 128, 128)
        scale = jnp.exp2(exps_ref[:, b:b + 1].astype(F32))
        zrows[0, 0, :, cols] = (codes_ref[:, cols].astype(F32) * scale).astype(BF16)
    zrows[1, 0] = grad_ref[...]
    pl.semaphore_wait(barrier, len(partners))

    def ring_copy(t, way, step):
        slot = step - 1 if way == 0 else (NZ - step + 1) % NZ
        there = step if way == 0 else NZ - step
        src, dst = zrows.at[t, PLACE[slot]], zrows.at[t, PLACE[there]]
        if step == NZ // 2:
            part = pl.ds(way * half_rows, half_rows)
            src, dst = src.at[part], dst.at[part]
        return remote(src, dst, ring_s.at[t, way, step - 1], ring_r.at[t, way, step - 1],
                      at_z(1 if way == 0 else NZ - 1))

    ring = [[[ring_copy(t, way, step) for step in range(1, 5)] for way in range(2)] for t in range(2)]

    def ring_start(t, step):
        for way in range(2):
            ring[t][way][step - 1].start()

    def ring_wait(t, step):
        for way in range(2):
            ring[t][way][step - 1].wait_recv()

    ring_start(0, 1)

    experts = meta_src.shape[0] * 8
    lanes = 4 * tokens
    expert_id = lax.broadcasted_iota(jnp.int32, (experts, lanes), 0)
    hit = jnp.zeros((experts, lanes), F32)
    weight = jnp.zeros((experts, lanes), F32)
    for k in range(routes_ref.shape[0]):
        same = routes_ref[k:k + 1, :] == expert_id
        hit = jnp.where(same, 1.0, hit)
        weight = jnp.where(same, rweight_ref[k:k + 1, :], weight)
    earlier = lax.broadcasted_iota(jnp.int32, (128, lanes), 0)
    later = lax.rem(lax.broadcasted_iota(jnp.int32, (128, lanes), 1), tokens)
    before = jnp.where((earlier < later) & (earlier < tokens), 1.0, 0.0).astype(BF16)
    count = dot_nn(hit[:, :128].astype(BF16), before)
    slots = jnp.where(hit > 0.5, count, -1.0)
    for g in range(NZ):
        meta_src[g, 0] = slots[g * 8:(g + 1) * 8]
        meta_src[g, 1] = weight[g * 8:(g + 1) * 8]
    meta_copies = []
    for k in range(1, NZ):
        copy = remote(meta_src.at[lax.rem(z + k, NZ)], meta.at[k], meta_s.at[k], meta_r.at[k], at_z(k))
        copy.start()
        meta_copies.append(copy)
    meta_own = pltpu.make_async_copy(meta_src.at[z], meta.at[0], meta_s.at[0])
    meta_own.start()

    weight_copies = []
    for m in range(3):
        copy = remote(weight_refs[m], weights.at[:, pl.ds(m * full + half, half)],
                      wt_s.at[m], wt_r.at[m], other_core)
        copy.start()
        weight_copies.append(copy)

    meta_own.wait()
    for copy in meta_copies:
        copy.wait_recv()

    lane_of = lax.broadcasted_iota(jnp.int32, (unit, lanes), 1)
    row_of = lax.broadcasted_iota(jnp.int32, (unit, lanes), 0)
    target = jnp.where(lax.div(lane_of, tokens) == lax.div(row_of, CAP), lax.rem(row_of, CAP), -5).astype(F32)
    source_of = lax.div(lax.broadcasted_iota(jnp.int32, (8, lanes), 1), tokens)
    for c in range(2):
        slot_cat = jnp.zeros((8, lanes), F32)
        weight_cat = jnp.zeros((8, lanes), F32)
        for q in range(4):
            slot_cat = jnp.where(source_of == q, meta[ORDER[4 * c + q], 0], slot_cat)
            weight_cat = jnp.where(source_of == q, meta[ORDER[4 * c + q], 1], weight_cat)
        for e in range(8):
            same = slot_cat[e:e + 1, :] == target
            weighted = jnp.where(same, weight_cat[e:e + 1, :], 0.0)
            span = pl.ds(e * unit, unit)
            pick[c, span, :] = jnp.where(same, 1.0, 0.0).astype(BF16)
            slot_w[c, span, :] = jnp.broadcast_to(jnp.sum(weighted, axis=1, keepdims=True), (unit, 128))
            act[0, span, pl.ds(0, lanes)] = weighted
            act[1, span, pl.ds(0, lanes)] = jnp.where(same, 1.0, 0.0)
        weighted_t = act[0, :, pl.ds(0, lanes)].T
        high = weighted_t.astype(BF16)
        pick_hi[c] = high
        pick_lo[c] = (weighted_t - high.astype(F32)).astype(BF16)
        pick_t[c] = act[1, :, pl.ds(0, lanes)].T.astype(BF16)

    disp = {}

    def dispatch(t, c):
        base = (t * 2 + c) * NX * 2

        def tile(n, carry):
            cols = cols_of(n)
            taken = zrows[t, pl.ds(4 * c, 4), :, cols].reshape(4 * tokens, TILE)
            chosen = dot_nn(pick[c], taken)
            if t == 1:
                chosen = chosen * slot_w[c][:, :1]
            sendrows[pl.ds(base, 2 * NX), :, cols] = chosen.astype(BF16).reshape(2 * NX, unit, TILE)
            return carry

        lax.fori_loop(0, tiles, tile, 0)
        for d in (2, 1, 3):
            copy = remote(sendrows.at[pl.ds(base + 2 * lax.rem(x + d, NX), 2)], arrived.at[t, :, c, d],
                          disp_s.at[t, c, d], disp_r.at[t, c, d], at_x(d))
            copy.start()
            disp[t, c, d] = copy
        copy = pltpu.make_async_copy(
            sendrows.at[pl.ds(base + 2 * x, 2)], arrived.at[t, :, c, 0], disp_s.at[t, c, 0])
        copy.start()
        disp[t, c, 0] = copy

    def dispatched(t):
        for c in range(2):
            disp[t, c, 0].wait()
            for d in range(1, NX):
                disp[t, c, d].wait_recv()

    ring_wait(0, 1)
    ring_start(0, 2)
    ring_start(1, 1)
    ring_wait(0, 2)
    ring_start(0, 3)
    dispatch(0, 0)
    ring_wait(1, 1)
    ring_start(1, 2)
    ring_wait(0, 3)
    ring_start(0, 4)
    ring_wait(1, 2)
    ring_start(1, 3)
    ring_wait(0, 4)
    dispatch(0, 1)
    dispatch(1, 0)
    ring_wait(1, 3)
    ring_start(1, 4)
    ring_wait(1, 4)
    dispatch(1, 1)

    for copy in own_copies:
        copy.wait()
    for copy in weight_copies:
        copy.wait_recv()

    ret = {}

    def send_back(t):
        for p in range(tiles):
            cols = pl.ds(p * TILE, TILE)
            for d in (2, 1, 3):
                copy = remote(results.at[t, :, :, d, :, cols], returned.at[t, x, :, :, :, cols],
                              ret_s.at[t, p, d], ret_r.at[t, p, d], at_x(NX - d))
                copy.start()
                ret[t, p, d] = copy
            copy = pltpu.make_async_copy(
                results.at[t, :, :, 0, :, cols], returned.at[t, x, :, :, :, cols], ret_s.at[t, p, 0])
            copy.start()
            ret[t, p, 0] = copy

    dispatched(0)

    def forward(j, carry):
        def project(n, carry):
            span = cols_of(n, 256)
            act[j, :, span] = dot_nt(arrived[0, j].reshape(rows, width), weights[j, span, :])
            return carry

        lax.fori_loop(0, 2 * full // 256, project, 0)
        gate = act[j, :, pl.ds(0, full)]
        sig = 1.0 / (1.0 + jnp.exp(-gate))
        hidden[j] = (gate * sig * act[j, :, pl.ds(full, full)]).astype(BF16)

        def down(n, carry):
            cols = cols_of(n)
            out = dot_nn(hidden[j], weights[j, pl.ds(2 * full, full), cols]).astype(BF16)
            results[0, j, :, :, :, cols] = out.reshape(2, NX, unit, TILE)
            return carry

        lax.fori_loop(0, tiles, down, 0)
        return carry

    lax.fori_loop(0, 2, forward, 0)
    send_back(0)

    dispatched(1)

    def backward(j, carry):
        back = dot_nt(arrived[1, j].reshape(rows, width), weights[j, pl.ds(2 * full, full), :])
        gate = act[j, :, pl.ds(0, full)]
        up = act[j, :, pl.ds(full, full)]
        sig = 1.0 / (1.0 + jnp.exp(-gate))
        grads[j, :, pl.ds(0, full)] = (back * up * sig * (1.0 + gate * (1.0 - sig))).astype(BF16)
        grads[j, :, pl.ds(full, full)] = (back * (gate * sig)).astype(BF16)

        def down(n, carry):
            cols = cols_of(n)
            out = dot_nn(grads[j], weights[j, pl.ds(0, 2 * full), cols]).astype(BF16)
            results[1, j, :, :, :, cols] = out.reshape(2, NX, unit, TILE)
            return carry

        lax.fori_loop(0, tiles, down, 0)
        return carry

    lax.fori_loop(0, 2, backward, 0)
    send_back(1)

    for copy in weight_copies:
        copy.wait_send()
    for t in range(2):
        for c in range(2):
            for d in range(1, NX):
                disp[t, c, d].wait_send()
    blocks = half // unit

    def weight_grads(j, carry):
        grads_t[...] = grads[j].T
        hidden_t[...] = hidden[j].T

        def tile(n, carry):
            cols = cols_of(n, 256)
            rows_in = arrived[0, j, :, :, :, cols].reshape(rows, 256)
            back_in = arrived[1, j, :, :, :, cols].reshape(rows, 256)
            for m in range(3):
                if m < 2:
                    total = dot_nn(grads_t[pl.ds(m * full, full), :], rows_in).astype(BF16)
                else:
                    total = dot_nn(hidden_t[...], back_in).astype(BF16)
                weights[j, pl.ds(m * full, half), cols] = total[:half]
                spot = pl.ds(m * 2 * blocks + j * blocks, blocks)
                sendrows[spot, :, cols] = total[half:].reshape(blocks, unit, 256)
            return carry

        lax.fori_loop(0, width // 256, tile, 0)
        return carry

    lax.fori_loop(0, 2, weight_grads, 0)
    wg_copies = []
    for m in range(3):
        spot = pl.ds(m * 2 * blocks, 2 * blocks)
        copy = remote(sendrows.at[spot], wrecv.at[spot], wg_s.at[m], wg_r.at[m], other_core)
        copy.start()
        wg_copies.append(copy)

    out_copies = []
    outs = (gate_out, up_out, down_out)

    def sum_replicas():
        for m in range(3):
            wg_copies[m].wait_recv()

            def tile(n, carry):
                cols = cols_of(n, 256)
                for j in range(2):
                    mine = weights[j, pl.ds(m * full, half), cols].astype(F32)
                    spot = pl.ds(m * 2 * blocks + j * blocks, blocks)
                    theirs = wrecv[spot, :, cols].reshape(half, 256).astype(F32)
                    weights[j, pl.ds(m * full, half), cols] = (mine + theirs).astype(BF16)
                return carry

            lax.fori_loop(0, width // 256, tile, 0)
            copy = pltpu.make_async_copy(
                weights.at[:, pl.ds(m * full, half)], outs[m], out_l.at[m])
            copy.start()
            out_copies.append(copy)

    for t in range(2):
        for way in range(2):
            for step in range(4):
                ring[t][way][step].wait_send()
    red = {}

    def reduce_copy(t, p, way, step):
        cols = pl.ds(p * TILE, TILE)
        if step == 1:
            spot, part = 1, pl.ds(way * half_rows, half_rows)
        else:
            spot, part = step + 3 * way, pl.ds(0, tokens)
        copy = remote(zrows.at[t, spot, part, cols], reduced.at[t, spot, part, cols],
                      red_s.at[t, p, way, step - 1], red_r.at[t, p, way, step - 1],
                      at_z(NZ - 1 if way == 0 else 1))
        red[t, p, way, step] = copy
        return copy

    def own_part(i, slot):
        return partial[i % 4, pl.ds(PLACE[slot] * tokens, tokens), :]

    def combine(i):
        t, p = divmod(i, tiles)
        cols = pl.ds(p * TILE, TILE)
        ret[t, p, 0].wait()
        for d in range(1, NX):
            ret[t, p, d].wait_recv()
        for c in range(2):
            back = returned[t, :, :, c, :, cols].reshape(rows, TILE)
            if t == 0:
                total = dot_nn(pick_hi[c], back) + dot_nn(pick_lo[c], back)
            else:
                total = dot_nn(pick_t[c], back)
            partial[i % 4, pl.ds(c * 4 * tokens, 4 * tokens), :] = total

    def reduce_step(i, step):
        t, p = divmod(i, tiles)
        cols = pl.ds(p * TILE, TILE)
        for way in range(2):
            slot = 5 - step if way == 0 else 3 + step
            mine = own_part(i, slot)
            if step == 1:
                part = pl.ds(way * half_rows, half_rows)
                zrows[t, 1, part, cols] = mine[way * half_rows:(way + 1) * half_rows].astype(BF16)
            else:
                red[t, p, way, step - 1].wait_recv()
                spot = step + 3 * way
                if step == 2:
                    part = pl.ds(way * half_rows, half_rows)
                    rest = pl.ds((1 - way) * half_rows, half_rows)
                    zrows[t, spot, part, cols] = (
                        mine[way * half_rows:(way + 1) * half_rows]
                        + reduced[t, 1, part, cols].astype(F32)).astype(BF16)
                    zrows[t, spot, rest, cols] = (
                        mine[(1 - way) * half_rows:(2 - way) * half_rows].astype(BF16))
                else:
                    zrows[t, spot, :, cols] = (
                        mine + reduced[t, spot - 1, :, cols].astype(F32)).astype(BF16)
            reduce_copy(t, p, way, step).start()

    hops = []

    def finish(i):
        t, p = divmod(i, tiles)
        cols = pl.ds(p * TILE, TILE)
        for way in range(2):
            red[t, p, way, 4].wait_recv()
        total = own_part(i, 0) + reduced[t, 4, :, cols].astype(F32) + reduced[t, 7, :, cols].astype(F32)
        final[t, :, cols] = (zrows[t, 0, :, cols].astype(F32) + total).astype(BF16)
        copy = remote(final.at[t, :, cols], (next_ref if t == 0 else prev_ref).at[:, cols],
                      hop_s.at[t, p], hop_r.at[t, p], sec_next if t == 0 else sec_prev)
        copy.start()
        hops.append(copy)

    items = 2 * tiles
    for i in range(items + 4):
        if i == 2:
            sum_replicas()
        if 0 <= i - 4:
            finish(i - 4)
        for step in (4, 3, 2):
            if 0 <= i - step + 1 < items:
                reduce_step(i - step + 1, step)
        if i < items:
            combine(i)
            reduce_step(i, 1)

    for copy in meta_copies:
        copy.wait_send()
    for copy in wg_copies:
        copy.wait_send()
    for t in range(2):
        for p in range(tiles):
            for d in range(1, NX):
                ret[t, p, d].wait_send()
    for copy in red.values():
        copy.wait_send()
    for copy in hops:
        copy.wait()
    for copy in out_copies:
        copy.wait()


def shards(
    row_codes, block_exponents, routes, route_weight, out_grad, gate_weight, up_weight, down_weight
):
    tokens, width = row_codes.shape[1:]
    local, half = gate_weight.shape[1:3]
    unit = 4 * CAP
    rows = NX * 2 * unit
    full = 2 * half
    tiles = width // TILE
    lanes = 4 * tokens
    routes_t = jnp.tile(routes[0].T, (1, 4))
    rweight_t = jnp.tile(route_weight[0].T, (1, 4))
    dma = pltpu.SemaphoreType.DMA
    any_spec = pl.BlockSpec(memory_space=pl.ANY)
    vmem_spec = pl.BlockSpec(memory_space=pltpu.VMEM)
    rows_type = jax.ShapeDtypeStruct((tokens, width), BF16)
    weight_type = jax.ShapeDtypeStruct((local, half, width), BF16)
    groups = NZ
    results = pl.pallas_call(
        kernel,
        out_shape=(rows_type, rows_type, weight_type, weight_type, weight_type),
        in_specs=[vmem_spec] * 5 + [any_spec] * 3,
        out_specs=[any_spec] * 5,
        scratch_shapes=[
            pltpu.VMEM((2, NZ, tokens, width), BF16),
            pltpu.VMEM((2 * 2 * NX * 2, unit, width), BF16),
            pltpu.VMEM((2, 2, 2, NX, unit, width), BF16),
            pltpu.VMEM((2, 3 * full, width), BF16),
            pltpu.VMEM((2, 2, 2, NX, unit, width), BF16),
            pltpu.VMEM((2, NX, 2, 2, unit, width), BF16),
            pltpu.VMEM((2, NZ, tokens, width), BF16),
            pltpu.VMEM((4, NZ * tokens, TILE), F32),
            pltpu.VMEM((3 * 2 * half // unit, unit, width), BF16),
            pltpu.VMEM((2, tokens, width), BF16),
            pltpu.VMEM((2, rows, 2 * full), F32),
            pltpu.VMEM((2, rows, full), BF16),
            pltpu.VMEM((full, rows), BF16),
            pltpu.VMEM((2, rows, 2 * full), BF16),
            pltpu.VMEM((2 * full, rows), BF16),
            pltpu.VMEM((groups, 2, 8, lanes), F32),
            pltpu.VMEM((groups, 2, 8, lanes), F32),
            pltpu.VMEM((2, rows, lanes), BF16),
            pltpu.VMEM((2, lanes, rows), BF16),
            pltpu.VMEM((2, lanes, rows), BF16),
            pltpu.VMEM((2, lanes, rows), BF16),
            pltpu.VMEM((2, rows, 128), F32),
            dma((2, 2, 4)), dma((2, 2, 4)),
            dma((NZ,)), dma((NZ,)),
            dma((3,)), dma((3,)), dma((3,)),
            dma((2, 2, NX)), dma((2, 2, NX)),
            dma((2, tiles, NX)), dma((2, tiles, NX)),
            dma((2, tiles, 2, 4)), dma((2, tiles, 2, 4)),
            dma((2, tiles)), dma((2, tiles)),
            dma((3,)), dma((3,)),
            dma((3,)),
        ],
        compiler_params=pltpu.CompilerParams(
            collective_id=0, has_side_effects=True, vmem_limit_bytes=62 * 2**20),
        cost_estimate=pl.CostEstimate(
            flops=12 * 10**9, bytes_accessed=16 * 10**6, transcendentals=10**6),
    )(
        row_codes[0], block_exponents[0], routes_t, rweight_t, out_grad[0],
        gate_weight[0], up_weight[0], down_weight[0],
    )
    return tuple(value[None] for value in results)


def solution(mesh):
    rows_spec = P("section", ("rep", "exp"), None)
    weight_spec = P("section", "exp", "rep", None)
    return jax.shard_map(
        shards,
        mesh=mesh,
        in_specs=(rows_spec,) * 5 + (weight_spec,) * 3,
        out_specs=(rows_spec,) * 2 + (weight_spec,) * 3,
        check_vma=False,
    )
```

```python
import functools

import jax
import jax.numpy as jnp
from jax import lax
from jax.experimental import pallas as pl
from jax.experimental.pallas import tpu as pltpu
from jax.sharding import PartitionSpec as P

MESH = pl.DeviceIdType.MESH
NX = 4
NZ = 8
CAP = 12
ORDER = (0, 1, 7, 2, 6, 3, 5, 4)
PLACE = tuple(ORDER.index(slot) for slot in range(NZ))
TILE = 512
BACK = tuple((0, start, TILE, False) for start in range(0, 2048, TILE)) + (
    (1, 0, 256, False), (1, 256, 512, False), (1, 768, 512, False), (1, 1280, 256, False),
    (1, 1536, 256, True), (1, 1792, 128, True), (1, 1920, 128, True))
AHEAD = 2
F32 = jnp.float32
BF16 = jnp.bfloat16


def dot_nn(a, b):
    return lax.dot_general(a, b, (((1,), (0,)), ((), ())), preferred_element_type=F32)


def dot_nt(a, b):
    return lax.dot_general(a, b, (((1,), (1,)), ((), ())), preferred_element_type=F32)


def kernel(
    codes_hbm, exps_hbm, routes_hbm, rweight_hbm, grad_hbm, gate_ref, up_ref, down_ref,
    next_ref, prev_ref, gate_out, up_out, down_out,
    codes_ref, exps_ref, routes_ref, rweight_ref, zrows, sendrows, arrived, weights, results, returned, reduced, partial, wrecv, final,
    act, hidden, hidden_t, grads, grads_t, meta_src, meta, pick, pick_t, pick_hi, pick_lo, slot_w,
    first_l, ring_s, ring_r, meta_s, meta_r, wt_l, wt_s, wt_r, disp_s, disp_r, ret_s, ret_r,
    red_s, red_r, hop_s, hop_r, wg_s, wg_r, out_l,
):
    tokens, width = codes_ref.shape
    unit = sendrows.shape[1]
    half_rows = tokens // 2
    rows = NX * 2 * unit
    half = gate_ref.shape[1]
    full = 2 * half
    tiles = width // TILE
    rep, sec, ex = lax.axis_index("rep"), lax.axis_index("section"), lax.axis_index("exp")
    sections = lax.axis_size("section")
    z, x = lax.div(ex, NX), lax.rem(ex, NX)

    def at_z(k):
        return (rep, sec, lax.rem(z + k, NZ) * NX + x)

    def at_x(k):
        return (rep, sec, z * NX + lax.rem(x + k, NX))

    other_core = (1 - rep, sec, ex)
    sec_next = (rep, lax.rem(sec + 1, sections), ex)
    sec_prev = (rep, lax.rem(sec + sections - 1, sections), ex)

    def remote(src, dst, send, recv, device):
        copy = pltpu.make_async_remote_copy(
            src_ref=src, dst_ref=dst, send_sem=send, recv_sem=recv,
            device_id=device, device_id_type=MESH)
        return copy

    def cols_of(n, size=TILE):
        return pl.ds(pl.multiple_of(n * size, size), size)

    first_copies = []
    for m, (src, dst) in enumerate((
            (exps_hbm, exps_ref), (codes_hbm, codes_ref), (routes_hbm, routes_ref),
            (rweight_hbm, rweight_ref), (grad_hbm, zrows.at[1, 0]))):
        copy = pltpu.make_async_copy(src, dst, first_l.at[m])
        copy.start()
        first_copies.append(copy)
    weight_refs = (gate_ref, up_ref, down_ref)
    own_copies = []
    for m in range(3):
        copy = pltpu.make_async_copy(
            weight_refs[m], weights.at[:, pl.ds(m * full, half)], wt_l.at[m])
        copy.start()
        own_copies.append(copy)
    partners = [at_z(k) for k in range(1, NZ)] + [at_x(k) for k in range(1, NX)]
    partners += [other_core, sec_next, sec_prev]
    barrier = pltpu.get_barrier_semaphore()
    for device in partners:
        pl.semaphore_signal(barrier, inc=1, device_id=device, device_id_type=MESH)

    first_copies[0].wait()
    first_copies[1].wait()
    scale = jnp.exp2(exps_ref[...].astype(F32)).astype(BF16)
    for p in range(tiles):
        cols = pl.ds(p * TILE, TILE)
        block = lax.broadcasted_iota(jnp.int32, (scale.shape[0], TILE), 1) + p * TILE
        chosen = jnp.where(
            lax.div(block, width // scale.shape[0])
            == lax.broadcasted_iota(jnp.int32, (scale.shape[0], TILE), 0), 1.0, 0.0).astype(BF16)
        wide = lax.dot_general(scale, chosen, (((0,), (0,)), ((), ())), preferred_element_type=F32)
        zrows[0, 0, :, cols] = (codes_ref[:, cols].astype(F32) * wide).astype(BF16)
    pl.semaphore_wait(barrier, len(partners))

    def ring_copy(i, way, step):
        t, p = divmod(i, tiles)
        cols = pl.ds(p * TILE, TILE)
        slot = step - 1 if way == 0 else (NZ - step + 1) % NZ
        there = step if way == 0 else NZ - step
        part = pl.ds(way * half_rows, half_rows) if step == NZ // 2 else pl.ds(0, tokens)
        return remote(zrows.at[t, PLACE[slot], part, cols], zrows.at[t, PLACE[there], part, cols],
                      ring_s.at[i, way, step - 1], ring_r.at[i, way, step - 1],
                      at_z(1 if way == 0 else NZ - 1))

    pieces = 2 * tiles
    ring = [[[ring_copy(i, way, step) for step in range(1, 5)] for way in range(2)] for i in range(pieces)]

    def ring_start(i, step):
        for way in range(2):
            if step > 1:
                ring[i][way][step - 2].wait_recv()
            ring[i][way][step - 1].start()

    ring_start(0, 1)
    ring_start(1, 1)
    first_copies[2].wait()
    first_copies[3].wait()
    experts = meta_src.shape[0] * 8
    lanes = 4 * tokens
    spread = jnp.where(
        lax.broadcasted_iota(jnp.int32, (tokens, lanes), 0)
        == lax.rem(lax.broadcasted_iota(jnp.int32, (tokens, lanes), 1), tokens), 1.0, 0.0).astype(BF16)
    routes_wide = dot_nn(routes_ref[...].astype(F32).astype(BF16), spread)
    rweight = rweight_ref[...]
    first = rweight.astype(BF16)
    rweight = rweight - first.astype(F32)
    second = rweight.astype(BF16)
    third = (rweight - second.astype(F32)).astype(BF16)
    rweight_wide = (dot_nn(first, spread) + dot_nn(second, spread)) + dot_nn(third, spread)
    expert_id = lax.broadcasted_iota(jnp.int32, (experts, lanes), 0).astype(F32)
    hit = jnp.zeros((experts, lanes), F32)
    weight = jnp.zeros((experts, lanes), F32)
    for k in range(routes_ref.shape[0]):
        same = routes_wide[k:k + 1, :] == expert_id
        hit = jnp.where(same, 1.0, hit)
        weight = jnp.where(same, rweight_wide[k:k + 1, :], weight)
    earlier = lax.broadcasted_iota(jnp.int32, (128, lanes), 0)
    later = lax.rem(lax.broadcasted_iota(jnp.int32, (128, lanes), 1), tokens)
    before = jnp.where((earlier < later) & (earlier < tokens), 1.0, 0.0).astype(BF16)
    count = dot_nn(hit[:, :128].astype(BF16), before)
    slots = jnp.where(hit > 0.5, count, -1.0)
    for g in range(NZ):
        meta_src[g, 0] = slots[g * 8:(g + 1) * 8]
        meta_src[g, 1] = weight[g * 8:(g + 1) * 8]

    meta_copies = []
    for k in range(1, NZ):
        copy = remote(meta_src.at[lax.rem(z + k, NZ)], meta.at[k], meta_s.at[k], meta_r.at[k], at_z(k))
        copy.start()
        meta_copies.append(copy)

    meta_own = pltpu.make_async_copy(meta_src.at[z], meta.at[0], meta_s.at[0])
    meta_own.start()

    weight_copies = []
    for m in range(3):
        copy = remote(weight_refs[m], weights.at[:, pl.ds(m * full + half, half)],
                      wt_s.at[m], wt_r.at[m], other_core)
        copy.start()
        weight_copies.append(copy)

    first_copies[4].wait()
    lane_of = lax.broadcasted_iota(jnp.int32, (unit, lanes), 1)
    row_of = lax.broadcasted_iota(jnp.int32, (unit, lanes), 0)
    target = jnp.where(lax.div(lane_of, tokens) == lax.div(row_of, CAP), lax.rem(row_of, CAP), -5).astype(F32)
    source_of = lax.div(lax.broadcasted_iota(jnp.int32, (8, lanes), 1), tokens)

    def gathered(c, which):
        found = jnp.zeros((8, lanes), F32)
        for q in range(4):
            found = jnp.where(source_of == q, meta[ORDER[4 * c + q], which], found)
        return found

    def make_pick(c):
        slot_cat = gathered(c, 0)
        for e in range(8):
            same = slot_cat[e:e + 1, :] == target
            pick[c, pl.ds(e * unit, unit), :] = jnp.where(same, 1.0, 0.0).astype(BF16)

    def make_weights(c):
        slot_cat, weight_cat = gathered(c, 0), gathered(c, 1)
        for e in range(8):
            same = slot_cat[e:e + 1, :] == target
            weighted = jnp.where(same, weight_cat[e:e + 1, :], 0.0)
            span = pl.ds(e * unit, unit)
            slot_w[c, span, :] = jnp.broadcast_to(jnp.sum(weighted, axis=1, keepdims=True), (unit, 128))
            act[c, span, pl.ds(0, lanes)] = weighted
            act[c, span, pl.ds(lanes, lanes)] = jnp.where(same, 1.0, 0.0)

    disp = {}

    def dispatch(i, c):
        t, p = divmod(i, tiles)
        cols = pl.ds(p * TILE, TILE)
        base = (t * 2 + c) * NX * 2
        taken = zrows[t, pl.ds(4 * c, 4), :, cols].reshape(4 * tokens, TILE)
        chosen = dot_nn(pick[c], taken)
        if t == 1:
            chosen = chosen * slot_w[c][:, :1]
        sendrows[pl.ds(base, 2 * NX), :, cols] = chosen.astype(BF16).reshape(2 * NX, unit, TILE)
        for d in (2, 1, 3):
            copy = remote(sendrows.at[pl.ds(base + 2 * lax.rem(x + d, NX), 2), :, cols],
                          arrived.at[t, :, c, d, :, cols],
                          disp_s.at[i, c, d], disp_r.at[i, c, d], at_x(d))
            copy.start()
            disp[i, c, d] = copy
        copy = pltpu.make_async_copy(
            sendrows.at[pl.ds(base + 2 * x, 2), :, cols], arrived.at[t, :, c, 0, :, cols],
            disp_s.at[i, c, 0])
        copy.start()
        disp[i, c, 0] = copy

    def dispatched(t):
        for i in range(t * tiles, (t + 1) * tiles):
            for c in range(2):
                disp[i, c, 0].wait()
                for d in range(1, NX):
                    disp[i, c, d].wait_recv()

    for turn in range(1, pieces + 4):
        for step in (4, 3, 2, 1):
            for i in range(pieces):
                if max(i, 1) - 2 + step == turn:
                    ring_start(i, step)
        if turn == 1:
            meta_own.wait()
            for copy in meta_copies:
                copy.wait_recv()
            make_pick(0)
        for i in range(pieces):
            if max(i, 1) + 3 == turn:
                for way in range(2):
                    ring[i][way][3].wait_recv()
                dispatch(i, 1)
        for i in range(pieces):
            if max(i, 1) + 1 == turn:
                dispatch(i, 0)
        if turn == 2:
            make_pick(1)
        if turn == 3:
            make_weights(0)
            make_weights(1)

    for c in range(2):
        weighted_t = act[c, :, pl.ds(0, lanes)].T
        high = weighted_t.astype(BF16)
        pick_hi[c] = high
        pick_lo[c] = (weighted_t - high.astype(F32)).astype(BF16)
        pick_t[c] = act[c, :, pl.ds(lanes, lanes)].T.astype(BF16)

    for copy in own_copies:
        copy.wait()
    for copy in weight_copies:
        copy.wait_recv()

    ret = {}

    def send_back(i):
        t, start, size, _ = BACK[i]
        cols = pl.ds(start, size)
        for d in (2, 1, 3):
            copy = remote(results.at[t, :, :, d, :, cols], returned.at[t, x, :, :, :, cols],
                          ret_s.at[i, d], ret_r.at[i, d], at_x(NX - d))
            copy.start()
            ret[i, d] = copy
        copy = pltpu.make_async_copy(
            results.at[t, :, :, 0, :, cols], returned.at[t, x, :, :, :, cols], ret_s.at[i, 0])
        copy.start()
        ret[i, 0] = copy

    dispatched(0)

    def forward(j, carry):
        def project(n, carry):
            span = cols_of(n, 256)
            act[j, :, span] = dot_nt(arrived[0, j].reshape(rows, width), weights[j, span, :])
            return carry

        lax.fori_loop(0, 2 * full // 256, project, 0)
        gate = act[j, :, pl.ds(0, full)]
        sig = 1.0 / (1.0 + jnp.exp(-gate))
        hidden[j] = (gate * sig * act[j, :, pl.ds(full, full)]).astype(BF16)

        def down(n, carry):
            cols = cols_of(n)
            out = dot_nn(hidden[j], weights[j, pl.ds(2 * full, full), cols]).astype(BF16)
            results[0, j, :, :, :, cols] = out.reshape(2, NX, unit, TILE)
            return carry

        lax.fori_loop(0, tiles, down, 0)
        return carry

    lax.fori_loop(0, 2, forward, 0)
    for i in range(tiles):
        send_back(i)

    dispatched(1)

    def backward(j, carry):
        back = dot_nt(arrived[1, j].reshape(rows, width), weights[j, pl.ds(2 * full, full), :])
        gate = act[j, :, pl.ds(0, full)]
        up = act[j, :, pl.ds(full, full)]
        sig = 1.0 / (1.0 + jnp.exp(-gate))
        grads[j, :, pl.ds(0, full)] = (back * up * sig * (1.0 + gate * (1.0 - sig))).astype(BF16)
        grads[j, :, pl.ds(full, full)] = (back * (gate * sig)).astype(BF16)

        def down(n, carry):
            cols = cols_of(n)
            out = dot_nn(grads[j], weights[j, pl.ds(0, 2 * full), cols]).astype(BF16)
            results[1, j, :, :, :, cols] = out.reshape(2, NX, unit, TILE)
            return carry

        lax.fori_loop(0, tiles, down, 0)
        return carry

    lax.fori_loop(0, 2, backward, 0)
    for i in range(tiles, tiles + AHEAD):
        send_back(i)

    for copy in weight_copies:
        copy.wait_send()
    for i in range(pieces):
        for c in range(2):
            for d in range(1, NX):
                disp[i, c, d].wait_send()
    blocks = half // unit

    def weight_grads(j, carry):
        grads_t[...] = grads[j].T
        hidden_t[...] = hidden[j].T

        def tile(n, carry):
            cols = cols_of(n, 256)
            rows_in = arrived[0, j, :, :, :, cols].reshape(rows, 256)
            back_in = arrived[1, j, :, :, :, cols].reshape(rows, 256)
            for m in range(3):
                if m < 2:
                    total = dot_nn(grads_t[pl.ds(m * full, full), :], rows_in).astype(BF16)
                else:
                    total = dot_nn(hidden_t[...], back_in).astype(BF16)
                weights[j, pl.ds(m * full, half), cols] = total[:half]
                spot = pl.ds(m * 2 * blocks + j * blocks, blocks)
                sendrows[spot, :, cols] = total[half:].reshape(blocks, unit, 256)
            return carry

        lax.fori_loop(0, width // 256, tile, 0)
        return carry

    lax.fori_loop(0, 2, weight_grads, 0)
    wg_copies = []
    for m in range(3):
        spot = pl.ds(m * 2 * blocks, 2 * blocks)
        copy = remote(sendrows.at[spot], wrecv.at[spot], wg_s.at[m], wg_r.at[m], other_core)
        copy.start()
        wg_copies.append(copy)

    out_copies = []
    outs = (gate_out, up_out, down_out)

    def sum_replicas():
        for m in range(3):
            wg_copies[m].wait_recv()

            def tile(n, carry):
                cols = cols_of(n, 256)
                for j in range(2):
                    mine = weights[j, pl.ds(m * full, half), cols].astype(F32)
                    spot = pl.ds(m * 2 * blocks + j * blocks, blocks)
                    theirs = wrecv[spot, :, cols].reshape(half, 256).astype(F32)
                    weights[j, pl.ds(m * full, half), cols] = (mine + theirs).astype(BF16)
                return carry

            lax.fori_loop(0, width // 256, tile, 0)
            copy = pltpu.make_async_copy(
                weights.at[:, pl.ds(m * full, half)], outs[m], out_l.at[m])
            copy.start()
            out_copies.append(copy)

    for i in range(pieces):
        for way in range(2):
            for step in range(4):
                ring[i][way][step].wait_send()
    red = {}

    def own_part(i, slot):
        return partial[i % 4, pl.ds(PLACE[slot] * tokens, tokens), pl.ds(0, BACK[i][2])]

    def combine(i):
        t, start, size, _ = BACK[i]
        cols = pl.ds(start, size)
        ret[i, 0].wait()
        for d in range(1, NX):
            ret[i, d].wait_recv()
        if tiles <= i < len(BACK) - AHEAD:
            send_back(i + AHEAD)
        for c in range(2):
            back = returned[t, :, :, c, :, cols].reshape(rows, size)
            if t == 0:
                total = dot_nn(pick_hi[c], back) + dot_nn(pick_lo[c], back)
            else:
                total = dot_nn(pick_t[c], back)
            partial[i % 4, pl.ds(c * 4 * tokens, 4 * tokens), pl.ds(0, size)] = total

    def reduce_start(i, spot, part, device, kind):
        t, start, size, _ = BACK[i]
        cols = pl.ds(start, size)
        copy = remote(zrows.at[t, spot[0], part, cols], reduced.at[t, spot[1], part, cols],
                      red_s.at[i, kind], red_r.at[i, kind], device)
        copy.start()
        red[i, kind] = copy

    def reduce_direct(i):
        t, start, size, _ = BACK[i]
        cols = pl.ds(start, size)
        for slot in (4, 3, 5, 2, 6, 1, 7):
            zrows[t, PLACE[slot], :, cols] = own_part(i, slot).astype(BF16)
            reduce_start(i, (PLACE[slot], slot), pl.ds(0, tokens), at_z(NZ - slot), slot)

    def reduce_step(i, step):
        t, start, size, _ = BACK[i]
        cols = pl.ds(start, size)
        for way in range(2):
            slot = 5 - step if way == 0 else 3 + step
            mine = own_part(i, slot)
            part, spot = pl.ds(0, tokens), step + 3 * way
            if step == 1:
                part, spot = pl.ds(way * half_rows, half_rows), 1
                zrows[t, 1, part, cols] = mine[way * half_rows:(way + 1) * half_rows].astype(BF16)
            else:
                red[i, way * 4 + step - 2].wait_recv()
                if step == 2:
                    got = pl.ds(way * half_rows, half_rows)
                    rest = pl.ds((1 - way) * half_rows, half_rows)
                    zrows[t, spot, got, cols] = (
                        mine[way * half_rows:(way + 1) * half_rows]
                        + reduced[t, 1, got, cols].astype(F32)).astype(BF16)
                    zrows[t, spot, rest, cols] = (
                        mine[(1 - way) * half_rows:(2 - way) * half_rows].astype(BF16))
                else:
                    zrows[t, spot, :, cols] = (
                        mine + reduced[t, spot - 1, :, cols].astype(F32)).astype(BF16)
            reduce_start(i, (spot, spot), part, at_z(NZ - 1 if way == 0 else 1), way * 4 + step - 1)

    hops = []

    def finish(i):
        t, start, size, direct = BACK[i]
        cols = pl.ds(start, size)
        total = own_part(i, 0)
        if direct:
            for slot in range(1, NZ):
                red[i, slot].wait_recv()
                total = total + reduced[t, slot, :, cols].astype(F32)
        else:
            for way in range(2):
                red[i, way * 4 + 3].wait_recv()
                total = total + reduced[t, 4 + 3 * way, :, cols].astype(F32)
        final[t, :, cols] = (zrows[t, 0, :, cols].astype(F32) + total).astype(BF16)
        copy = remote(final.at[t, :, cols], (next_ref if t == 0 else prev_ref).at[:, cols],
                      hop_s.at[i], hop_r.at[i], sec_next if t == 0 else sec_prev)
        copy.start()
        hops.append(copy)

    items = len(BACK)
    ended = 0
    for turn in range(items + 4):
        if turn == 2:
            sum_replicas()
        while ended < items and (turn >= ended + 4 or turn >= items and BACK[ended][3]):
            finish(ended)
            ended += 1
        for step in (4, 3, 2):
            i = turn - step + 1
            if 0 <= i < items and not BACK[i][3]:
                reduce_step(i, step)
        if turn < items:
            combine(turn)
            if BACK[turn][3]:
                reduce_direct(turn)
            else:
                reduce_step(turn, 1)

    for copy in meta_copies:
        copy.wait_send()
    for copy in wg_copies:
        copy.wait_send()
    for i in range(items):
        for d in range(1, NX):
            ret[i, d].wait_send()
    for copy in red.values():
        copy.wait_send()
    for copy in hops:
        copy.wait()
    for copy in out_copies:
        copy.wait()


def place_kernel(*refs):
    sems_in, sems_out = refs[-2:]
    held = refs[:-2]
    count = len(held) // 3
    inward, outward = [], []
    for m in range(count):
        source, target, middle = held[m], held[count + m], held[2 * count + m]
        parts = 2 if len(source.shape) == 3 else 1
        for h in range(parts):
            view = [ref.at[h] if parts == 2 else ref for ref in (source, target, middle)]
            inward.append(pltpu.make_async_copy(view[0], view[2], sems_in.at[m, h]))
            outward.append(pltpu.make_async_copy(view[2], view[1], sems_out.at[m, h]))
            inward[-1].start()
    for first, second in zip(inward, outward):
        first.wait()
        second.start()
    for copy in outward:
        copy.wait()


def shards(
    row_codes, block_exponents, routes, route_weight, out_grad, gate_weight, up_weight, down_weight
):
    tokens, width = row_codes.shape[1:]
    local, half = gate_weight.shape[1:3]
    unit = 4 * CAP
    rows = NX * 2 * unit
    full = 2 * half
    tiles = width // TILE
    lanes = 4 * tokens
    dma = pltpu.SemaphoreType.DMA
    any_spec = pl.BlockSpec(memory_space=pl.ANY)
    rows_type = jax.ShapeDtypeStruct((tokens, width), BF16)
    weight_type = jax.ShapeDtypeStruct((local, half, width), BF16)
    groups = NZ
    results = pl.pallas_call(
        kernel,
        out_shape=(rows_type, rows_type, weight_type, weight_type, weight_type),
        in_specs=[any_spec] * 8,
        out_specs=[any_spec] * 5,
        scratch_shapes=[
            pltpu.VMEM((tokens, width), BF16),
            pltpu.VMEM((block_exponents.shape[2], tokens), jnp.int32),
            pltpu.VMEM((routes.shape[2], tokens), jnp.int32),
            pltpu.VMEM((routes.shape[2], tokens), F32),
            pltpu.VMEM((2, NZ, tokens, width), BF16),
            pltpu.VMEM((2 * 2 * NX * 2, unit, width), BF16),
            pltpu.VMEM((2, 2, 2, NX, unit, width), BF16),
            pltpu.VMEM((2, 3 * full, width), BF16),
            pltpu.VMEM((2, 2, 2, NX, unit, width), BF16),
            pltpu.VMEM((2, NX, 2, 2, unit, width), BF16),
            pltpu.VMEM((2, NZ, tokens, width), BF16),
            pltpu.VMEM((4, NZ * tokens, TILE), F32),
            pltpu.VMEM((3 * 2 * half // unit, unit, width), BF16),
            pltpu.VMEM((2, tokens, width), BF16),
            pltpu.VMEM((2, rows, 2 * full), F32),
            pltpu.VMEM((2, rows, full), BF16),
            pltpu.VMEM((full, rows), BF16),
            pltpu.VMEM((2, rows, 2 * full), BF16),
            pltpu.VMEM((2 * full, rows), BF16),
            pltpu.VMEM((groups, 2, 8, lanes), F32),
            pltpu.VMEM((groups, 2, 8, lanes), F32),
            pltpu.VMEM((2, rows, lanes), BF16),
            pltpu.VMEM((2, lanes, rows), BF16),
            pltpu.VMEM((2, lanes, rows), BF16),
            pltpu.VMEM((2, lanes, rows), BF16),
            pltpu.VMEM((2, rows, 128), F32),
            dma((5,)),
            dma((2 * tiles, 2, 4)), dma((2 * tiles, 2, 4)),
            dma((NZ,)), dma((NZ,)),
            dma((3,)), dma((3,)), dma((3,)),
            dma((2 * tiles, 2, NX)), dma((2 * tiles, 2, NX)),
            dma((len(BACK), NX)), dma((len(BACK), NX)),
            dma((len(BACK), 8)), dma((len(BACK), 8)),
            dma((len(BACK),)), dma((len(BACK),)),
            dma((3,)), dma((3,)),
            dma((3,)),
        ],
        compiler_params=pltpu.CompilerParams(
            collective_id=0, has_side_effects=True, vmem_limit_bytes=62 * 2**20),
        cost_estimate=pl.CostEstimate(
            flops=12 * 10**9, bytes_accessed=16 * 10**6, transcendentals=10**6),
    )(
        row_codes[0], block_exponents[0].T, routes[0].T, route_weight[0].T, out_grad[0],
        gate_weight[0], up_weight[0], down_weight[0],
    )
    results = pl.pallas_call(
        place_kernel,
        out_shape=tuple(jax.ShapeDtypeStruct(value.shape, value.dtype) for value in results),
        in_specs=[any_spec] * 5,
        out_specs=[any_spec] * 5,
        scratch_shapes=[pltpu.VMEM(value.shape, value.dtype) for value in results] + [dma((5, 2)), dma((5, 2))],
        compiler_params=pltpu.CompilerParams(vmem_limit_bytes=62 * 2**20),
    )(*results)
    return tuple(value[None] for value in results)


def solution(mesh):
    rows_spec = P("section", ("rep", "exp"), None)
    weight_spec = P("section", "exp", "rep", None)
    return jax.shard_map(
        shards,
        mesh=mesh,
        in_specs=(rows_spec,) * 5 + (weight_spec,) * 3,
        out_specs=(rows_spec,) * 2 + (weight_spec,) * 3,
        check_vma=False,
    )
```

```python
import functools

import jax
import jax.numpy as jnp
from jax import lax
from jax.experimental import pallas as pl
from jax.experimental.pallas import tpu as pltpu
from jax.sharding import PartitionSpec as P

MESH = pl.DeviceIdType.MESH
NX = 4
NZ = 8
CAP = 12
ORDER = (0, 1, 7, 2, 6, 3, 5, 4)
PLACE = tuple(ORDER.index(slot) for slot in range(NZ))
TILE = 512
BACK = tuple((0, start, TILE, False) for start in range(0, 2048, TILE)) + (
    (1, 0, 256, False), (1, 256, 512, False), (1, 768, 512, False), (1, 1280, 256, False),
    (1, 1536, 256, False), (1, 1792, 256, True))
AHEAD = 2
F32 = jnp.float32
BF16 = jnp.bfloat16


def dot_nn(a, b):
    return lax.dot_general(a, b, (((1,), (0,)), ((), ())), preferred_element_type=F32)


def dot_nt(a, b):
    return lax.dot_general(a, b, (((1,), (1,)), ((), ())), preferred_element_type=F32)


def kernel(
    codes_hbm, exps_hbm, routes_hbm, rweight_hbm, grad_hbm, gate_ref, up_ref, down_ref,
    next_ref, prev_ref, gate_out, up_out, down_out,
    codes_ref, exps_ref, routes_ref, rweight_ref, zrows, sendrows, arrived, weights, results, returned, reduced, partial, wrecv, final,
    act, hidden, hidden_t, grads, grads_t, meta_src, meta, pick, pick_t, pick_hi, pick_lo, slot_w,
    first_l, ring_s, ring_r, meta_s, meta_r, wt_l, wt_s, wt_r, disp_s, disp_r, ret_s, ret_r,
    red_s, red_r, hop_s, hop_r, wg_s, wg_r, out_l,
):
    tokens, width = codes_ref.shape
    unit = sendrows.shape[1]
    half_rows = tokens // 2
    rows = NX * 2 * unit
    half = gate_ref.shape[1]
    full = 2 * half
    tiles = width // TILE
    rep, sec, ex = lax.axis_index("rep"), lax.axis_index("section"), lax.axis_index("exp")
    sections = lax.axis_size("section")
    z, x = lax.div(ex, NX), lax.rem(ex, NX)

    def at_z(k):
        return (rep, sec, lax.rem(z + k, NZ) * NX + x)

    def at_x(k):
        return (rep, sec, z * NX + lax.rem(x + k, NX))

    other_core = (1 - rep, sec, ex)
    sec_next = (rep, lax.rem(sec + 1, sections), ex)
    sec_prev = (rep, lax.rem(sec + sections - 1, sections), ex)

    def remote(src, dst, send, recv, device):
        copy = pltpu.make_async_remote_copy(
            src_ref=src, dst_ref=dst, send_sem=send, recv_sem=recv,
            device_id=device, device_id_type=MESH)
        return copy

    def cols_of(n, size=TILE):
        return pl.ds(pl.multiple_of(n * size, size), size)

    first_copies = []
    for m, (src, dst) in enumerate((
            (exps_hbm, exps_ref), (codes_hbm, codes_ref), (routes_hbm, routes_ref),
            (rweight_hbm, rweight_ref), (grad_hbm, zrows.at[1, 0]))):
        copy = pltpu.make_async_copy(src, dst, first_l.at[m])
        copy.start()
        first_copies.append(copy)
    weight_refs = (gate_ref, up_ref, down_ref)
    own_copies = []
    for m in range(3):
        copy = pltpu.make_async_copy(
            weight_refs[m], weights.at[:, pl.ds(m * full, half)], wt_l.at[m])
        copy.start()
        own_copies.append(copy)
    partners = [at_z(k) for k in range(1, NZ)] + [at_x(k) for k in range(1, NX)]
    partners += [other_core, sec_next, sec_prev]
    barrier = pltpu.get_barrier_semaphore()
    for device in partners:
        pl.semaphore_signal(barrier, inc=1, device_id=device, device_id_type=MESH)

    first_copies[0].wait()
    first_copies[1].wait()
    scale = jnp.exp2(exps_ref[...].astype(F32)).astype(BF16)

    def scale_rows(p):
        cols = pl.ds(p * TILE, TILE)
        block = lax.broadcasted_iota(jnp.int32, (scale.shape[0], TILE), 1) + p * TILE
        chosen = jnp.where(
            lax.div(block, width // scale.shape[0])
            == lax.broadcasted_iota(jnp.int32, (scale.shape[0], TILE), 0), 1.0, 0.0).astype(BF16)
        wide = lax.dot_general(scale, chosen, (((0,), (0,)), ((), ())), preferred_element_type=F32)
        zrows[0, 0, :, cols] = (codes_ref[:, cols].astype(F32) * wide).astype(BF16)
    scale_rows(0)
    scale_rows(1)
    pl.semaphore_wait(barrier, len(partners))

    def ring_copy(i, way, step):
        t, p = divmod(i, tiles)
        cols = pl.ds(p * TILE, TILE)
        slot = step - 1 if way == 0 else (NZ - step + 1) % NZ
        there = step if way == 0 else NZ - step
        part = pl.ds(way * half_rows, half_rows) if step == NZ // 2 else pl.ds(0, tokens)
        return remote(zrows.at[t, PLACE[slot], part, cols], zrows.at[t, PLACE[there], part, cols],
                      ring_s.at[i, way, step - 1], ring_r.at[i, way, step - 1],
                      at_z(1 if way == 0 else NZ - 1))

    pieces = 2 * tiles
    ring = [[[ring_copy(i, way, step) for step in range(1, 5)] for way in range(2)] for i in range(pieces)]

    def ring_start(i, step):
        for way in range(2):
            if step > 1:
                ring[i][way][step - 2].wait_recv()
            ring[i][way][step - 1].start()

    ring_start(0, 1)
    ring_start(1, 1)
    for p in range(2, tiles):
        scale_rows(p)
    first_copies[2].wait()
    first_copies[3].wait()
    experts = meta_src.shape[0] * 8
    lanes = 4 * tokens
    spread = jnp.where(
        lax.broadcasted_iota(jnp.int32, (tokens, lanes), 0)
        == lax.rem(lax.broadcasted_iota(jnp.int32, (tokens, lanes), 1), tokens), 1.0, 0.0).astype(BF16)
    routes_wide = dot_nn(routes_ref[...].astype(F32).astype(BF16), spread)
    rweight = rweight_ref[...]
    first = rweight.astype(BF16)
    rweight = rweight - first.astype(F32)
    second = rweight.astype(BF16)
    third = (rweight - second.astype(F32)).astype(BF16)
    rweight_wide = (dot_nn(first, spread) + dot_nn(second, spread)) + dot_nn(third, spread)
    expert_id = lax.broadcasted_iota(jnp.int32, (experts, lanes), 0).astype(F32)
    hit = jnp.zeros((experts, lanes), F32)
    weight = jnp.zeros((experts, lanes), F32)
    for k in range(routes_ref.shape[0]):
        same = routes_wide[k:k + 1, :] == expert_id
        hit = jnp.where(same, 1.0, hit)
        weight = jnp.where(same, rweight_wide[k:k + 1, :], weight)
    earlier = lax.broadcasted_iota(jnp.int32, (128, lanes), 0)
    later = lax.rem(lax.broadcasted_iota(jnp.int32, (128, lanes), 1), tokens)
    before = jnp.where((earlier < later) & (earlier < tokens), 1.0, 0.0).astype(BF16)
    count = dot_nn(hit[:, :128].astype(BF16), before)
    slots = jnp.where(hit > 0.5, count, -1.0)
    for g in range(NZ):
        meta_src[g, 0] = slots[g * 8:(g + 1) * 8]
        meta_src[g, 1] = weight[g * 8:(g + 1) * 8]

    meta_copies = []
    for k in range(1, NZ):
        copy = remote(meta_src.at[lax.rem(z + k, NZ)], meta.at[k], meta_s.at[k], meta_r.at[k], at_z(k))
        copy.start()
        meta_copies.append(copy)

    meta_own = pltpu.make_async_copy(meta_src.at[z], meta.at[0], meta_s.at[0])
    meta_own.start()

    weight_copies = []
    for m in range(3):
        copy = remote(weight_refs[m], weights.at[:, pl.ds(m * full + half, half)],
                      wt_s.at[m], wt_r.at[m], other_core)
        copy.start()
        weight_copies.append(copy)

    first_copies[4].wait()
    lane_of = lax.broadcasted_iota(jnp.int32, (unit, lanes), 1)
    row_of = lax.broadcasted_iota(jnp.int32, (unit, lanes), 0)
    target = jnp.where(lax.div(lane_of, tokens) == lax.div(row_of, CAP), lax.rem(row_of, CAP), -5).astype(F32)
    source_of = lax.div(lax.broadcasted_iota(jnp.int32, (8, lanes), 1), tokens)

    def gathered(c, which):
        found = jnp.zeros((8, lanes), F32)
        for q in range(4):
            found = jnp.where(source_of == q, meta[ORDER[4 * c + q], which], found)
        return found

    def make_pick(c):
        slot_cat = gathered(c, 0)
        for e in range(8):
            same = slot_cat[e:e + 1, :] == target
            pick[c, pl.ds(e * unit, unit), :] = jnp.where(same, 1.0, 0.0).astype(BF16)

    def make_weights(c):
        slot_cat, weight_cat = gathered(c, 0), gathered(c, 1)
        for e in range(8):
            same = slot_cat[e:e + 1, :] == target
            weighted = jnp.where(same, weight_cat[e:e + 1, :], 0.0)
            span = pl.ds(e * unit, unit)
            slot_w[c, span, :] = jnp.broadcast_to(jnp.sum(weighted, axis=1, keepdims=True), (unit, 128))
            act[c, span, pl.ds(0, lanes)] = weighted
            act[c, span, pl.ds(lanes, lanes)] = jnp.where(same, 1.0, 0.0)

    disp = {}

    def dispatch(i, c):
        t, p = divmod(i, tiles)
        cols = pl.ds(p * TILE, TILE)
        base = (t * 2 + c) * NX * 2
        taken = zrows[t, pl.ds(4 * c, 4), :, cols].reshape(4 * tokens, TILE)
        chosen = dot_nn(pick[c], taken)
        if t == 1:
            chosen = chosen * slot_w[c][:, :1]
        sendrows[pl.ds(base, 2 * NX), :, cols] = chosen.astype(BF16).reshape(2 * NX, unit, TILE)
        for d in (2, 1, 3):
            copy = remote(sendrows.at[pl.ds(base + 2 * lax.rem(x + d, NX), 2), :, cols],
                          arrived.at[t, :, c, d, :, cols],
                          disp_s.at[i, c, d], disp_r.at[i, c, d], at_x(d))
            copy.start()
            disp[i, c, d] = copy
        copy = pltpu.make_async_copy(
            sendrows.at[pl.ds(base + 2 * x, 2), :, cols], arrived.at[t, :, c, 0, :, cols],
            disp_s.at[i, c, 0])
        copy.start()
        disp[i, c, 0] = copy

    def dispatched(t):
        for i in range(t * tiles, (t + 1) * tiles):
            for c in range(2):
                disp[i, c, 0].wait()
                for d in range(1, NX):
                    disp[i, c, d].wait_recv()

    for turn in range(1, pieces + 4):
        for step in (4, 3, 2, 1):
            for i in range(pieces):
                if max(i, 1) - 2 + step == turn:
                    ring_start(i, step)
                    if step == 3:
                        dispatch(i, 0)
        if turn == 1:
            meta_own.wait()
            for copy in meta_copies:
                copy.wait_recv()
            make_pick(0)
        for i in range(pieces):
            if max(i, 1) + 3 == turn:
                for way in range(2):
                    ring[i][way][3].wait_recv()
                dispatch(i, 1)
        if turn == 2:
            make_pick(1)
        if turn == 3:
            make_weights(0)
            make_weights(1)

    for c in range(2):
        weighted_t = act[c, :, pl.ds(0, lanes)].T
        high = weighted_t.astype(BF16)
        pick_hi[c] = high
        pick_lo[c] = (weighted_t - high.astype(F32)).astype(BF16)
        pick_t[c] = act[c, :, pl.ds(lanes, lanes)].T.astype(BF16)

    for copy in own_copies:
        copy.wait()
    for copy in weight_copies:
        copy.wait_recv()

    ret = {}

    def send_back(i):
        t, start, size, _ = BACK[i]
        cols = pl.ds(start, size)
        for d in (2, 1, 3):
            copy = remote(results.at[t, :, :, d, :, cols], returned.at[t, x, :, :, :, cols],
                          ret_s.at[i, d], ret_r.at[i, d], at_x(NX - d))
            copy.start()
            ret[i, d] = copy
        copy = pltpu.make_async_copy(
            results.at[t, :, :, 0, :, cols], returned.at[t, x, :, :, :, cols], ret_s.at[i, 0])
        copy.start()
        ret[i, 0] = copy

    dispatched(0)

    def forward(j, carry):
        def project(n, carry):
            span = cols_of(n, 256)
            act[j, :, span] = dot_nt(arrived[0, j].reshape(rows, width), weights[j, span, :])
            return carry

        lax.fori_loop(0, 2 * full // 256, project, 0)
        gate = act[j, :, pl.ds(0, full)]
        sig = 1.0 / (1.0 + jnp.exp(-gate))
        hidden[j] = (gate * sig * act[j, :, pl.ds(full, full)]).astype(BF16)

        def down(n, carry):
            cols = cols_of(n)
            out = dot_nn(hidden[j], weights[j, pl.ds(2 * full, full), cols]).astype(BF16)
            results[0, j, :, :, :, cols] = out.reshape(2, NX, unit, TILE)
            return carry

        lax.fori_loop(0, tiles, down, 0)
        return carry

    lax.fori_loop(0, 2, forward, 0)
    for i in range(tiles):
        send_back(i)

    dispatched(1)

    def backward(j, carry):
        back = dot_nt(arrived[1, j].reshape(rows, width), weights[j, pl.ds(2 * full, full), :])
        gate = act[j, :, pl.ds(0, full)]
        up = act[j, :, pl.ds(full, full)]
        sig = 1.0 / (1.0 + jnp.exp(-gate))
        grads[j, :, pl.ds(0, full)] = (back * up * sig * (1.0 + gate * (1.0 - sig))).astype(BF16)
        grads[j, :, pl.ds(full, full)] = (back * (gate * sig)).astype(BF16)

        def down(n, carry):
            cols = cols_of(n)
            out = dot_nn(grads[j], weights[j, pl.ds(0, 2 * full), cols]).astype(BF16)
            results[1, j, :, :, :, cols] = out.reshape(2, NX, unit, TILE)
            return carry

        lax.fori_loop(0, tiles, down, 0)
        return carry

    lax.fori_loop(0, 2, backward, 0)
    for i in range(tiles, tiles + AHEAD):
        send_back(i)

    for copy in weight_copies:
        copy.wait_send()
    for i in range(pieces):
        for c in range(2):
            for d in range(1, NX):
                disp[i, c, d].wait_send()
    blocks = half // unit

    def weight_grads(j, carry):
        grads_t[...] = grads[j].T
        hidden_t[...] = hidden[j].T

        def tile(n, carry):
            cols = cols_of(n, 256)
            rows_in = arrived[0, j, :, :, :, cols].reshape(rows, 256)
            back_in = arrived[1, j, :, :, :, cols].reshape(rows, 256)
            for m in range(3):
                if m < 2:
                    total = dot_nn(grads_t[pl.ds(m * full, full), :], rows_in).astype(BF16)
                else:
                    total = dot_nn(hidden_t[...], back_in).astype(BF16)
                weights[j, pl.ds(m * full, half), cols] = total[:half]
                spot = pl.ds(m * 2 * blocks + j * blocks, blocks)
                sendrows[spot, :, cols] = total[half:].reshape(blocks, unit, 256)
            return carry

        lax.fori_loop(0, width // 256, tile, 0)
        return carry

    lax.fori_loop(0, 2, weight_grads, 0)
    wg_copies = []
    for m in range(3):
        spot = pl.ds(m * 2 * blocks, 2 * blocks)
        copy = remote(sendrows.at[spot], wrecv.at[spot], wg_s.at[m], wg_r.at[m], other_core)
        copy.start()
        wg_copies.append(copy)

    out_copies = []
    outs = (gate_out, up_out, down_out)

    def sum_replicas():
        for m in range(3):
            wg_copies[m].wait_recv()

            def tile(n, carry):
                cols = cols_of(n, 256)
                for j in range(2):
                    mine = weights[j, pl.ds(m * full, half), cols].astype(F32)
                    spot = pl.ds(m * 2 * blocks + j * blocks, blocks)
                    theirs = wrecv[spot, :, cols].reshape(half, 256).astype(F32)
                    weights[j, pl.ds(m * full, half), cols] = (mine + theirs).astype(BF16)
                return carry

            lax.fori_loop(0, width // 256, tile, 0)
            copy = pltpu.make_async_copy(
                weights.at[:, pl.ds(m * full, half)], outs[m], out_l.at[m])
            copy.start()
            out_copies.append(copy)

    for i in range(pieces):
        for way in range(2):
            for step in range(4):
                ring[i][way][step].wait_send()
    red = {}

    def own_part(i, slot):
        return partial[i % 4, pl.ds(PLACE[slot] * tokens, tokens), pl.ds(0, BACK[i][2])]

    def combine(i):
        t, start, size, _ = BACK[i]
        cols = pl.ds(start, size)
        ret[i, 0].wait()
        for d in range(1, NX):
            ret[i, d].wait_recv()
        if tiles <= i < len(BACK) - AHEAD:
            send_back(i + AHEAD)
        for c in range(2):
            back = returned[t, :, :, c, :, cols].reshape(rows, size)
            if t == 0:
                total = dot_nn(pick_hi[c], back) + dot_nn(pick_lo[c], back)
            else:
                total = dot_nn(pick_t[c], back)
            partial[i % 4, pl.ds(c * 4 * tokens, 4 * tokens), pl.ds(0, size)] = total

    def reduce_start(i, spot, part, device, kind):
        t, start, size, _ = BACK[i]
        cols = pl.ds(start, size)
        copy = remote(zrows.at[t, spot[0], part, cols], reduced.at[t, spot[1], part, cols],
                      red_s.at[i, kind], red_r.at[i, kind], device)
        copy.start()
        red[i, kind] = copy

    def reduce_direct(i):
        t, start, size, _ = BACK[i]
        cols = pl.ds(start, size)
        for slot in (4, 3, 5, 2, 6, 1, 7):
            zrows[t, PLACE[slot], :, cols] = own_part(i, slot).astype(BF16)
            reduce_start(i, (PLACE[slot], slot), pl.ds(0, tokens), at_z(NZ - slot), slot)

    def reduce_step(i, step):
        t, start, size, _ = BACK[i]
        cols = pl.ds(start, size)
        for way in range(2):
            slot = 5 - step if way == 0 else 3 + step
            mine = own_part(i, slot)
            part, spot = pl.ds(0, tokens), step + 3 * way
            if step == 1:
                part, spot = pl.ds(way * half_rows, half_rows), 1
                zrows[t, 1, part, cols] = mine[way * half_rows:(way + 1) * half_rows].astype(BF16)
            else:
                red[i, way * 4 + step - 2].wait_recv()
                if step == 2:
                    got = pl.ds(way * half_rows, half_rows)
                    rest = pl.ds((1 - way) * half_rows, half_rows)
                    zrows[t, spot, got, cols] = (
                        mine[way * half_rows:(way + 1) * half_rows]
                        + reduced[t, 1, got, cols].astype(F32)).astype(BF16)
                    zrows[t, spot, rest, cols] = (
                        mine[(1 - way) * half_rows:(2 - way) * half_rows].astype(BF16))
                else:
                    zrows[t, spot, :, cols] = (
                        mine + reduced[t, spot - 1, :, cols].astype(F32)).astype(BF16)
            reduce_start(i, (spot, spot), part, at_z(NZ - 1 if way == 0 else 1), way * 4 + step - 1)

    hops = []

    def finish(i):
        t, start, size, direct = BACK[i]
        cols = pl.ds(start, size)
        total = own_part(i, 0)
        if direct:
            for slot in range(1, NZ):
                red[i, slot].wait_recv()
                total = total + reduced[t, slot, :, cols].astype(F32)
        else:
            for way in range(2):
                red[i, way * 4 + 3].wait_recv()
                total = total + reduced[t, 4 + 3 * way, :, cols].astype(F32)
        final[t, :, cols] = (zrows[t, 0, :, cols].astype(F32) + total).astype(BF16)
        copy = remote(final.at[t, :, cols], (next_ref if t == 0 else prev_ref).at[:, cols],
                      hop_s.at[i], hop_r.at[i], sec_next if t == 0 else sec_prev)
        copy.start()
        hops.append(copy)

    items = len(BACK)
    ended = 0
    for turn in range(items + 4):
        if turn == 2:
            sum_replicas()
        while ended < items and (turn >= ended + 4 or turn >= items and BACK[ended][3]):
            finish(ended)
            ended += 1
        for step in (4, 3, 2):
            i = turn - step + 1
            if 0 <= i < items and not BACK[i][3]:
                reduce_step(i, step)
        if turn < items:
            combine(turn)
            if BACK[turn][3]:
                reduce_direct(turn)
            else:
                reduce_step(turn, 1)

    for copy in meta_copies:
        copy.wait_send()
    for copy in wg_copies:
        copy.wait_send()
    for i in range(items):
        for d in range(1, NX):
            ret[i, d].wait_send()
    for copy in red.values():
        copy.wait_send()
    for copy in hops:
        copy.wait()
    for copy in out_copies:
        copy.wait()


def place_kernel(*refs):
    sems_in, sems_out = refs[-2:]
    held = refs[:-2]
    count = len(held) // 3
    inward, outward = [], []
    for m in range(count):
        source, target, middle = held[m], held[count + m], held[2 * count + m]
        parts = 2 if len(source.shape) == 3 else 1
        for h in range(parts):
            if parts == 1:
                view = (source, target, middle)
            else:
                view = [ref.at[h] for ref in (source, target, middle)]
            inward.append(pltpu.make_async_copy(view[0], view[2], sems_in.at[m, h]))
            outward.append(pltpu.make_async_copy(view[2], view[1], sems_out.at[m, h]))
            inward[-1].start()
    for first, second in zip(inward, outward):
        first.wait()
        second.start()
    for copy in outward:
        copy.wait()


def shards(
    row_codes, block_exponents, routes, route_weight, out_grad, gate_weight, up_weight, down_weight
):
    tokens, width = row_codes.shape[1:]
    local, half = gate_weight.shape[1:3]
    unit = 4 * CAP
    rows = NX * 2 * unit
    full = 2 * half
    tiles = width // TILE
    lanes = 4 * tokens
    dma = pltpu.SemaphoreType.DMA
    any_spec = pl.BlockSpec(memory_space=pl.ANY)
    rows_type = jax.ShapeDtypeStruct((tokens, width), BF16)
    weight_type = jax.ShapeDtypeStruct((local, half, width), BF16)
    groups = NZ
    results = pl.pallas_call(
        kernel,
        out_shape=(rows_type, rows_type, weight_type, weight_type, weight_type),
        in_specs=[any_spec] * 8,
        out_specs=[any_spec] * 5,
        scratch_shapes=[
            pltpu.VMEM((tokens, width), BF16),
            pltpu.VMEM((block_exponents.shape[2], tokens), jnp.int32),
            pltpu.VMEM((routes.shape[2], tokens), jnp.int32),
            pltpu.VMEM((routes.shape[2], tokens), F32),
            pltpu.VMEM((2, NZ, tokens, width), BF16),
            pltpu.VMEM((2 * 2 * NX * 2, unit, width), BF16),
            pltpu.VMEM((2, 2, 2, NX, unit, width), BF16),
            pltpu.VMEM((2, 3 * full, width), BF16),
            pltpu.VMEM((2, 2, 2, NX, unit, width), BF16),
            pltpu.VMEM((2, NX, 2, 2, unit, width), BF16),
            pltpu.VMEM((2, NZ, tokens, width), BF16),
            pltpu.VMEM((4, NZ * tokens, TILE), F32),
            pltpu.VMEM((3 * 2 * half // unit, unit, width), BF16),
            pltpu.VMEM((2, tokens, width), BF16),
            pltpu.VMEM((2, rows, 2 * full), F32),
            pltpu.VMEM((2, rows, full), BF16),
            pltpu.VMEM((full, rows), BF16),
            pltpu.VMEM((2, rows, 2 * full), BF16),
            pltpu.VMEM((2 * full, rows), BF16),
            pltpu.VMEM((groups, 2, 8, lanes), F32),
            pltpu.VMEM((groups, 2, 8, lanes), F32),
            pltpu.VMEM((2, rows, lanes), BF16),
            pltpu.VMEM((2, lanes, rows), BF16),
            pltpu.VMEM((2, lanes, rows), BF16),
            pltpu.VMEM((2, lanes, rows), BF16),
            pltpu.VMEM((2, rows, 128), F32),
            dma((5,)),
            dma((2 * tiles, 2, 4)), dma((2 * tiles, 2, 4)),
            dma((NZ,)), dma((NZ,)),
            dma((3,)), dma((3,)), dma((3,)),
            dma((2 * tiles, 2, NX)), dma((2 * tiles, 2, NX)),
            dma((len(BACK), NX)), dma((len(BACK), NX)),
            dma((len(BACK), 8)), dma((len(BACK), 8)),
            dma((len(BACK),)), dma((len(BACK),)),
            dma((3,)), dma((3,)),
            dma((3,)),
        ],
        compiler_params=pltpu.CompilerParams(
            collective_id=0, has_side_effects=True, vmem_limit_bytes=62 * 2**20),
        cost_estimate=pl.CostEstimate(
            flops=12 * 10**9, bytes_accessed=16 * 10**6, transcendentals=10**6),
    )(
        row_codes[0], block_exponents[0].T, routes[0].T, route_weight[0].T, out_grad[0],
        gate_weight[0], up_weight[0], down_weight[0],
    )
    results = pl.pallas_call(
        place_kernel,
        out_shape=tuple(jax.ShapeDtypeStruct(value.shape, value.dtype) for value in results),
        in_specs=[any_spec] * 5,
        out_specs=[any_spec] * 5,
        scratch_shapes=[pltpu.VMEM(value.shape, value.dtype) for value in results] + [dma((5, 2)), dma((5, 2))],
        compiler_params=pltpu.CompilerParams(vmem_limit_bytes=62 * 2**20),
    )(*results)
    return tuple(value[None] for value in results)


def solution(mesh):
    rows_spec = P("section", ("rep", "exp"), None)
    weight_spec = P("section", "exp", "rep", None)
    return jax.shard_map(
        shards,
        mesh=mesh,
        in_specs=(rows_spec,) * 5 + (weight_spec,) * 3,
        out_specs=(rows_spec,) * 2 + (weight_spec,) * 3,
        check_vma=False,
    )
```

```python
import functools

import jax
import jax.numpy as jnp
from jax import lax
from jax.experimental import pallas as pl
from jax.experimental.pallas import tpu as pltpu
from jax.sharding import PartitionSpec as P

MESH = pl.DeviceIdType.MESH
NX = 4
NZ = 8
CAP = 12
ORDER = (0, 1, 7, 2, 6, 3, 5, 4)
PLACE = tuple(ORDER.index(slot) for slot in range(NZ))
TILE = 512
BACK = tuple((0, start, TILE, False) for start in range(0, 2048, TILE)) + (
    (1, 0, 256, False), (1, 256, 512, False), (1, 768, 512, False), (1, 1280, 256, False),
    (1, 1536, 256, False), (1, 1792, 256, True))
AHEAD = 3
F32 = jnp.float32
BF16 = jnp.bfloat16


def dot_nn(a, b):
    return lax.dot_general(a, b, (((1,), (0,)), ((), ())), preferred_element_type=F32)


def dot_nt(a, b):
    return lax.dot_general(a, b, (((1,), (1,)), ((), ())), preferred_element_type=F32)


def kernel(
    codes_hbm, exps_hbm, routes_hbm, rweight_hbm, grad_hbm, gate_ref, up_ref, down_ref,
    next_ref, prev_ref, gate_out, up_out, down_out,
    codes_ref, exps_ref, routes_ref, rweight_ref, zrows, sendrows, arrived, weights, results, returned, reduced, partial, wrecv, final,
    act, hidden, hidden_t, grads, grads_t, meta_src, meta, pick, pick_t, pick_hi, pick_lo, slot_w,
    first_l, ring_s, ring_r, meta_s, meta_r, wt_l, wt_s, wt_r, disp_s, disp_r, ret_s, ret_r,
    red_s, red_r, hop_s, hop_r, wg_s, wg_r, out_l,
):
    tokens, width = codes_ref.shape
    unit = sendrows.shape[1]
    half_rows = tokens // 2
    rows = NX * 2 * unit
    half = gate_ref.shape[1]
    full = 2 * half
    tiles = width // TILE
    rep, sec, ex = lax.axis_index("rep"), lax.axis_index("section"), lax.axis_index("exp")
    sections = lax.axis_size("section")
    z, x = lax.div(ex, NX), lax.rem(ex, NX)

    def at_z(k):
        return (rep, sec, lax.rem(z + k, NZ) * NX + x)

    def at_x(k):
        return (rep, sec, z * NX + lax.rem(x + k, NX))

    other_core = (1 - rep, sec, ex)
    sec_next = (rep, lax.rem(sec + 1, sections), ex)
    sec_prev = (rep, lax.rem(sec + sections - 1, sections), ex)

    def remote(src, dst, send, recv, device):
        copy = pltpu.make_async_remote_copy(
            src_ref=src, dst_ref=dst, send_sem=send, recv_sem=recv,
            device_id=device, device_id_type=MESH)
        return copy

    def cols_of(n, size=TILE):
        return pl.ds(pl.multiple_of(n * size, size), size)

    first_copies = []
    for m, (src, dst) in enumerate((
            (exps_hbm, exps_ref), (codes_hbm, codes_ref), (routes_hbm, routes_ref),
            (rweight_hbm, rweight_ref), (grad_hbm, zrows.at[1, 0]))):
        copy = pltpu.make_async_copy(src, dst, first_l.at[m])
        copy.start()
        first_copies.append(copy)
    weight_refs = (gate_ref, up_ref, down_ref)
    own_copies = []
    for m in range(3):
        copy = pltpu.make_async_copy(
            weight_refs[m], weights.at[:, pl.ds(m * full, half)], wt_l.at[m])
        copy.start()
        own_copies.append(copy)
    partners = [at_z(k) for k in range(1, NZ)] + [at_x(k) for k in range(1, NX)]
    partners += [other_core, sec_next, sec_prev]
    barrier = pltpu.get_barrier_semaphore()
    for device in partners:
        pl.semaphore_signal(barrier, inc=1, device_id=device, device_id_type=MESH)

    first_copies[0].wait()
    first_copies[1].wait()
    scale = jnp.exp2(exps_ref[...].astype(F32)).astype(BF16)

    def scale_rows(p):
        cols = pl.ds(p * TILE, TILE)
        block = lax.broadcasted_iota(jnp.int32, (scale.shape[0], TILE), 1) + p * TILE
        chosen = jnp.where(
            lax.div(block, width // scale.shape[0])
            == lax.broadcasted_iota(jnp.int32, (scale.shape[0], TILE), 0), 1.0, 0.0).astype(BF16)
        wide = lax.dot_general(scale, chosen, (((0,), (0,)), ((), ())), preferred_element_type=F32)
        zrows[0, 0, :, cols] = (codes_ref[:, cols].astype(F32) * wide).astype(BF16)
    scale_rows(0)
    scale_rows(1)
    pl.semaphore_wait(barrier, len(partners))

    def ring_copy(i, way, step):
        t, p = divmod(i, tiles)
        cols = pl.ds(p * TILE, TILE)
        slot = step - 1 if way == 0 else (NZ - step + 1) % NZ
        there = step if way == 0 else NZ - step
        part = pl.ds(way * half_rows, half_rows) if step == NZ // 2 else pl.ds(0, tokens)
        return remote(zrows.at[t, PLACE[slot], part, cols], zrows.at[t, PLACE[there], part, cols],
                      ring_s.at[i, way, step - 1], ring_r.at[i, way, step - 1],
                      at_z(1 if way == 0 else NZ - 1))

    pieces = 2 * tiles
    ring = [[[ring_copy(i, way, step) for step in range(1, 5)] for way in range(2)] for i in range(pieces)]

    def ring_start(i, step):
        for way in range(2):
            if step > 1:
                ring[i][way][step - 2].wait_recv()
            ring[i][way][step - 1].start()

    ring_start(0, 1)
    ring_start(1, 1)
    for p in range(2, tiles):
        scale_rows(p)
    first_copies[2].wait()
    first_copies[3].wait()
    experts = meta_src.shape[0] * 8
    lanes = 4 * tokens
    spread = jnp.where(
        lax.broadcasted_iota(jnp.int32, (tokens, lanes), 0)
        == lax.rem(lax.broadcasted_iota(jnp.int32, (tokens, lanes), 1), tokens), 1.0, 0.0).astype(BF16)
    routes_wide = dot_nn(routes_ref[...].astype(F32).astype(BF16), spread)
    rweight = rweight_ref[...]
    first = rweight.astype(BF16)
    rweight = rweight - first.astype(F32)
    second = rweight.astype(BF16)
    third = (rweight - second.astype(F32)).astype(BF16)
    rweight_wide = (dot_nn(first, spread) + dot_nn(second, spread)) + dot_nn(third, spread)
    expert_id = lax.broadcasted_iota(jnp.int32, (experts, lanes), 0).astype(F32)
    hit = jnp.zeros((experts, lanes), F32)
    weight = jnp.zeros((experts, lanes), F32)
    for k in range(routes_ref.shape[0]):
        same = routes_wide[k:k + 1, :] == expert_id
        hit = jnp.where(same, 1.0, hit)
        weight = jnp.where(same, rweight_wide[k:k + 1, :], weight)
    earlier = lax.broadcasted_iota(jnp.int32, (128, lanes), 0)
    later = lax.rem(lax.broadcasted_iota(jnp.int32, (128, lanes), 1), tokens)
    before = jnp.where((earlier < later) & (earlier < tokens), 1.0, 0.0).astype(BF16)
    count = dot_nn(hit[:, :128].astype(BF16), before)
    slots = jnp.where(hit > 0.5, count, -1.0)
    for g in range(NZ):
        meta_src[g, 0] = slots[g * 8:(g + 1) * 8]
        meta_src[g, 1] = weight[g * 8:(g + 1) * 8]

    meta_copies = []
    for k in range(1, NZ):
        copy = remote(meta_src.at[lax.rem(z + k, NZ)], meta.at[k], meta_s.at[k], meta_r.at[k], at_z(k))
        copy.start()
        meta_copies.append(copy)

    meta_own = pltpu.make_async_copy(meta_src.at[z], meta.at[0], meta_s.at[0])
    meta_own.start()

    weight_copies = []
    for m in range(3):
        copy = remote(weight_refs[m], weights.at[:, pl.ds(m * full + half, half)],
                      wt_s.at[m], wt_r.at[m], other_core)
        copy.start()
        weight_copies.append(copy)

    first_copies[4].wait()
    lane_of = lax.broadcasted_iota(jnp.int32, (unit, lanes), 1)
    row_of = lax.broadcasted_iota(jnp.int32, (unit, lanes), 0)
    target = jnp.where(lax.div(lane_of, tokens) == lax.div(row_of, CAP), lax.rem(row_of, CAP), -5).astype(F32)
    source_of = lax.div(lax.broadcasted_iota(jnp.int32, (8, lanes), 1), tokens)

    def gathered(c, which):
        found = jnp.zeros((8, lanes), F32)
        for q in range(4):
            found = jnp.where(source_of == q, meta[ORDER[4 * c + q], which], found)
        return found

    def make_pick(c):
        slot_cat = gathered(c, 0)
        for e in range(8):
            same = slot_cat[e:e + 1, :] == target
            pick[c, pl.ds(e * unit, unit), :] = jnp.where(same, 1.0, 0.0).astype(BF16)

    def make_weights(c):
        slot_cat, weight_cat = gathered(c, 0), gathered(c, 1)
        for e in range(8):
            same = slot_cat[e:e + 1, :] == target
            weighted = jnp.where(same, weight_cat[e:e + 1, :], 0.0)
            span = pl.ds(e * unit, unit)
            slot_w[c, span, :] = jnp.broadcast_to(jnp.sum(weighted, axis=1, keepdims=True), (unit, 128))
            act[c, span, pl.ds(0, lanes)] = weighted
            act[c, span, pl.ds(lanes, lanes)] = jnp.where(same, 1.0, 0.0)

    disp = {}

    def dispatch(i, c):
        t, p = divmod(i, tiles)
        cols = pl.ds(p * TILE, TILE)
        base = (t * 2 + c) * NX * 2
        taken = zrows[t, pl.ds(4 * c, 4), :, cols].reshape(4 * tokens, TILE)
        chosen = dot_nn(pick[c], taken)
        if t == 1:
            chosen = chosen * slot_w[c][:, :1]
        sendrows[pl.ds(base, 2 * NX), :, cols] = chosen.astype(BF16).reshape(2 * NX, unit, TILE)
        for d in (2, 1, 3):
            copy = remote(sendrows.at[pl.ds(base + 2 * lax.rem(x + d, NX), 2), :, cols],
                          arrived.at[t, :, c, d, :, cols],
                          disp_s.at[i, c, d], disp_r.at[i, c, d], at_x(d))
            copy.start()
            disp[i, c, d] = copy
        copy = pltpu.make_async_copy(
            sendrows.at[pl.ds(base + 2 * x, 2), :, cols], arrived.at[t, :, c, 0, :, cols],
            disp_s.at[i, c, 0])
        copy.start()
        disp[i, c, 0] = copy

    def dispatched(t):
        for i in range(t * tiles, (t + 1) * tiles):
            for c in range(2):
                disp[i, c, 0].wait()
                for d in range(1, NX):
                    disp[i, c, d].wait_recv()

    for turn in range(1, pieces + 4):
        for step in (4, 3, 2, 1):
            for i in range(pieces):
                if max(i, 1) - 2 + step == turn:
                    ring_start(i, step)
                    if step == 3:
                        dispatch(i, 0)
        if turn == 1:
            meta_own.wait()
            for copy in meta_copies:
                copy.wait_recv()
            make_pick(0)
        for i in range(pieces):
            if max(i, 1) + 3 == turn:
                for way in range(2):
                    ring[i][way][3].wait_recv()
                dispatch(i, 1)
        if turn == 2:
            make_pick(1)
        if turn == 3:
            make_weights(0)
            make_weights(1)

    for c in range(2):
        weighted_t = act[c, :, pl.ds(0, lanes)].T
        high = weighted_t.astype(BF16)
        pick_hi[c] = high
        pick_lo[c] = (weighted_t - high.astype(F32)).astype(BF16)
        pick_t[c] = act[c, :, pl.ds(lanes, lanes)].T.astype(BF16)

    for copy in own_copies:
        copy.wait()
    for copy in weight_copies:
        copy.wait_recv()

    ret = {}

    def send_back(i):
        t, start, size, _ = BACK[i]
        cols = pl.ds(start, size)
        for d in (2, 1, 3):
            copy = remote(results.at[t, :, :, d, :, cols], returned.at[t, x, :, :, :, cols],
                          ret_s.at[i, d], ret_r.at[i, d], at_x(NX - d))
            copy.start()
            ret[i, d] = copy
        copy = pltpu.make_async_copy(
            results.at[t, :, :, 0, :, cols], returned.at[t, x, :, :, :, cols], ret_s.at[i, 0])
        copy.start()
        ret[i, 0] = copy

    dispatched(0)

    def forward(j, carry):
        def project(n, carry):
            span = cols_of(n, 256)
            act[j, :, span] = dot_nt(arrived[0, j].reshape(rows, width), weights[j, span, :])
            return carry

        lax.fori_loop(0, 2 * full // 256, project, 0)
        gate = act[j, :, pl.ds(0, full)]
        sig = 1.0 / (1.0 + jnp.exp(-gate))
        hidden[j] = (gate * sig * act[j, :, pl.ds(full, full)]).astype(BF16)

        def down(n, carry):
            cols = cols_of(n)
            out = dot_nn(hidden[j], weights[j, pl.ds(2 * full, full), cols]).astype(BF16)
            results[0, j, :, :, :, cols] = out.reshape(2, NX, unit, TILE)
            return carry

        lax.fori_loop(0, tiles, down, 0)
        return carry

    lax.fori_loop(0, 2, forward, 0)
    for i in range(tiles):
        send_back(i)

    dispatched(1)

    def backward(j, carry):
        back = dot_nt(arrived[1, j].reshape(rows, width), weights[j, pl.ds(2 * full, full), :])
        gate = act[j, :, pl.ds(0, full)]
        up = act[j, :, pl.ds(full, full)]
        sig = 1.0 / (1.0 + jnp.exp(-gate))
        grads[j, :, pl.ds(0, full)] = (back * up * sig * (1.0 + gate * (1.0 - sig))).astype(BF16)
        grads[j, :, pl.ds(full, full)] = (back * (gate * sig)).astype(BF16)

        def down(n, carry):
            cols = cols_of(n)
            out = dot_nn(grads[j], weights[j, pl.ds(0, 2 * full), cols]).astype(BF16)
            results[1, j, :, :, :, cols] = out.reshape(2, NX, unit, TILE)
            return carry

        lax.fori_loop(0, tiles, down, 0)
        return carry

    lax.fori_loop(0, 2, backward, 0)
    for i in range(tiles, tiles + AHEAD):
        send_back(i)

    for copy in weight_copies:
        copy.wait_send()
    for i in range(pieces):
        for c in range(2):
            for d in range(1, NX):
                disp[i, c, d].wait_send()
    blocks = half // unit

    def weight_grads(j, carry):
        grads_t[...] = grads[j].T
        hidden_t[...] = hidden[j].T

        def tile(n, carry):
            cols = cols_of(n, 256)
            rows_in = arrived[0, j, :, :, :, cols].reshape(rows, 256)
            back_in = arrived[1, j, :, :, :, cols].reshape(rows, 256)
            for m in range(3):
                if m < 2:
                    total = dot_nn(grads_t[pl.ds(m * full, full), :], rows_in).astype(BF16)
                else:
                    total = dot_nn(hidden_t[...], back_in).astype(BF16)
                weights[j, pl.ds(m * full, half), cols] = total[:half]
                spot = pl.ds(m * 2 * blocks + j * blocks, blocks)
                sendrows[spot, :, cols] = total[half:].reshape(blocks, unit, 256)
            return carry

        lax.fori_loop(0, width // 256, tile, 0)
        return carry

    lax.fori_loop(0, 2, weight_grads, 0)
    wg_copies = []
    for m in range(3):
        spot = pl.ds(m * 2 * blocks, 2 * blocks)
        copy = remote(sendrows.at[spot], wrecv.at[spot], wg_s.at[m], wg_r.at[m], other_core)
        copy.start()
        wg_copies.append(copy)

    out_copies = []
    outs = (gate_out, up_out, down_out)

    def sum_replicas():
        for m in range(3):
            wg_copies[m].wait_recv()

            def tile(n, carry):
                cols = cols_of(n, 256)
                for j in range(2):
                    mine = weights[j, pl.ds(m * full, half), cols].astype(F32)
                    spot = pl.ds(m * 2 * blocks + j * blocks, blocks)
                    theirs = wrecv[spot, :, cols].reshape(half, 256).astype(F32)
                    weights[j, pl.ds(m * full, half), cols] = (mine + theirs).astype(BF16)
                return carry

            lax.fori_loop(0, width // 256, tile, 0)
            copy = pltpu.make_async_copy(
                weights.at[:, pl.ds(m * full, half)], outs[m], out_l.at[m])
            copy.start()
            out_copies.append(copy)

    for i in range(pieces):
        for way in range(2):
            for step in range(4):
                ring[i][way][step].wait_send()
    red = {}

    def own_part(i, slot):
        return partial[i % 4, pl.ds(PLACE[slot] * tokens, tokens), pl.ds(0, BACK[i][2])]

    def combine(i):
        t, start, size, _ = BACK[i]
        cols = pl.ds(start, size)
        ret[i, 0].wait()
        for d in range(1, NX):
            ret[i, d].wait_recv()
        if tiles <= i < len(BACK) - AHEAD:
            send_back(i + AHEAD)
        for c in range(2):
            back = returned[t, :, :, c, :, cols].reshape(rows, size)
            if t == 0:
                total = dot_nn(pick_hi[c], back) + dot_nn(pick_lo[c], back)
            else:
                total = dot_nn(pick_t[c], back)
            partial[i % 4, pl.ds(c * 4 * tokens, 4 * tokens), pl.ds(0, size)] = total

    def reduce_start(i, spot, part, device, kind):
        t, start, size, _ = BACK[i]
        cols = pl.ds(start, size)
        copy = remote(zrows.at[t, spot[0], part, cols], reduced.at[t, spot[1], part, cols],
                      red_s.at[i, kind], red_r.at[i, kind], device)
        copy.start()
        red[i, kind] = copy

    def reduce_direct(i):
        t, start, size, _ = BACK[i]
        cols = pl.ds(start, size)
        for slot in (4, 3, 5, 2, 6, 1, 7):
            zrows[t, PLACE[slot], :, cols] = own_part(i, slot).astype(BF16)
            reduce_start(i, (PLACE[slot], slot), pl.ds(0, tokens), at_z(NZ - slot), slot)

    def reduce_step(i, step):
        t, start, size, _ = BACK[i]
        cols = pl.ds(start, size)
        for way in range(2):
            slot = 5 - step if way == 0 else 3 + step
            mine = own_part(i, slot)
            part, spot = pl.ds(0, tokens), step + 3 * way
            if step == 1:
                part, spot = pl.ds(way * half_rows, half_rows), 1
                zrows[t, 1, part, cols] = mine[way * half_rows:(way + 1) * half_rows].astype(BF16)
            else:
                red[i, way * 4 + step - 2].wait_recv()
                if step == 2:
                    got = pl.ds(way * half_rows, half_rows)
                    rest = pl.ds((1 - way) * half_rows, half_rows)
                    zrows[t, spot, got, cols] = (
                        mine[way * half_rows:(way + 1) * half_rows]
                        + reduced[t, 1, got, cols].astype(F32)).astype(BF16)
                    zrows[t, spot, rest, cols] = (
                        mine[(1 - way) * half_rows:(2 - way) * half_rows].astype(BF16))
                else:
                    zrows[t, spot, :, cols] = (
                        mine + reduced[t, spot - 1, :, cols].astype(F32)).astype(BF16)
            reduce_start(i, (spot, spot), part, at_z(NZ - 1 if way == 0 else 1), way * 4 + step - 1)

    hops = []

    def finish(i):
        t, start, size, direct = BACK[i]
        cols = pl.ds(start, size)
        total = own_part(i, 0)
        if direct:
            for slot in range(1, NZ):
                red[i, slot].wait_recv()
                total = total + reduced[t, slot, :, cols].astype(F32)
        else:
            for way in range(2):
                red[i, way * 4 + 3].wait_recv()
                total = total + reduced[t, 4 + 3 * way, :, cols].astype(F32)
        final[t, :, cols] = (zrows[t, 0, :, cols].astype(F32) + total).astype(BF16)
        copy = remote(final.at[t, :, cols], (next_ref if t == 0 else prev_ref).at[:, cols],
                      hop_s.at[i], hop_r.at[i], sec_next if t == 0 else sec_prev)
        copy.start()
        hops.append(copy)

    items = len(BACK)
    ended = 0
    for turn in range(items + 4):
        if turn == 2:
            sum_replicas()
        while ended < items and (turn >= ended + 4 or turn >= items and BACK[ended][3]):
            finish(ended)
            ended += 1
        for step in (4, 3, 2):
            i = turn - step + 1
            if 0 <= i < items and not BACK[i][3]:
                reduce_step(i, step)
        if turn < items:
            combine(turn)
            if BACK[turn][3]:
                reduce_direct(turn)
            else:
                reduce_step(turn, 1)

    for copy in meta_copies:
        copy.wait_send()
    for copy in wg_copies:
        copy.wait_send()
    for i in range(items):
        for d in range(1, NX):
            ret[i, d].wait_send()
    for copy in red.values():
        copy.wait_send()
    for copy in hops:
        copy.wait()
    for copy in out_copies:
        copy.wait()


def place_kernel(*refs):
    sems_in, sems_out = refs[-2:]
    held = refs[:-2]
    count = len(held) // 3
    inward, outward = [], []
    for m in range(count):
        source, target, middle = held[m], held[count + m], held[2 * count + m]
        parts = 2 if len(source.shape) == 3 else 1
        for h in range(parts):
            if parts == 1:
                view = (source, target, middle)
            else:
                view = [ref.at[h] for ref in (source, target, middle)]
            inward.append(pltpu.make_async_copy(view[0], view[2], sems_in.at[m, h]))
            outward.append(pltpu.make_async_copy(view[2], view[1], sems_out.at[m, h]))
            inward[-1].start()
    for first, second in zip(inward, outward):
        first.wait()
        second.start()
    for copy in outward:
        copy.wait()


def shards(
    row_codes, block_exponents, routes, route_weight, out_grad, gate_weight, up_weight, down_weight
):
    tokens, width = row_codes.shape[1:]
    local, half = gate_weight.shape[1:3]
    unit = 4 * CAP
    rows = NX * 2 * unit
    full = 2 * half
    tiles = width // TILE
    lanes = 4 * tokens
    dma = pltpu.SemaphoreType.DMA
    any_spec = pl.BlockSpec(memory_space=pl.ANY)
    rows_type = jax.ShapeDtypeStruct((tokens, width), BF16)
    weight_type = jax.ShapeDtypeStruct((local, half, width), BF16)
    groups = NZ
    results = pl.pallas_call(
        kernel,
        out_shape=(rows_type, rows_type, weight_type, weight_type, weight_type),
        in_specs=[any_spec] * 8,
        out_specs=[any_spec] * 5,
        scratch_shapes=[
            pltpu.VMEM((tokens, width), BF16),
            pltpu.VMEM((block_exponents.shape[2], tokens), jnp.int32),
            pltpu.VMEM((routes.shape[2], tokens), jnp.int32),
            pltpu.VMEM((routes.shape[2], tokens), F32),
            pltpu.VMEM((2, NZ, tokens, width), BF16),
            pltpu.VMEM((2 * 2 * NX * 2, unit, width), BF16),
            pltpu.VMEM((2, 2, 2, NX, unit, width), BF16),
            pltpu.VMEM((2, 3 * full, width), BF16),
            pltpu.VMEM((2, 2, 2, NX, unit, width), BF16),
            pltpu.VMEM((2, NX, 2, 2, unit, width), BF16),
            pltpu.VMEM((2, NZ, tokens, width), BF16),
            pltpu.VMEM((4, NZ * tokens, TILE), F32),
            pltpu.VMEM((3 * 2 * half // unit, unit, width), BF16),
            pltpu.VMEM((2, tokens, width), BF16),
            pltpu.VMEM((2, rows, 2 * full), F32),
            pltpu.VMEM((2, rows, full), BF16),
            pltpu.VMEM((full, rows), BF16),
            pltpu.VMEM((2, rows, 2 * full), BF16),
            pltpu.VMEM((2 * full, rows), BF16),
            pltpu.VMEM((groups, 2, 8, lanes), F32),
            pltpu.VMEM((groups, 2, 8, lanes), F32),
            pltpu.VMEM((2, rows, lanes), BF16),
            pltpu.VMEM((2, lanes, rows), BF16),
            pltpu.VMEM((2, lanes, rows), BF16),
            pltpu.VMEM((2, lanes, rows), BF16),
            pltpu.VMEM((2, rows, 128), F32),
            dma((5,)),
            dma((2 * tiles, 2, 4)), dma((2 * tiles, 2, 4)),
            dma((NZ,)), dma((NZ,)),
            dma((3,)), dma((3,)), dma((3,)),
            dma((2 * tiles, 2, NX)), dma((2 * tiles, 2, NX)),
            dma((len(BACK), NX)), dma((len(BACK), NX)),
            dma((len(BACK), 8)), dma((len(BACK), 8)),
            dma((len(BACK),)), dma((len(BACK),)),
            dma((3,)), dma((3,)),
            dma((3,)),
        ],
        compiler_params=pltpu.CompilerParams(
            collective_id=0, has_side_effects=True, vmem_limit_bytes=62 * 2**20),
        cost_estimate=pl.CostEstimate(
            flops=12 * 10**9, bytes_accessed=16 * 10**6, transcendentals=10**6),
    )(
        row_codes[0], block_exponents[0].T, routes[0].T, route_weight[0].T, out_grad[0],
        gate_weight[0], up_weight[0], down_weight[0],
    )
    results = pl.pallas_call(
        place_kernel,
        out_shape=tuple(jax.ShapeDtypeStruct(value.shape, value.dtype) for value in results),
        in_specs=[any_spec] * 5,
        out_specs=[any_spec] * 5,
        scratch_shapes=[pltpu.VMEM(value.shape, value.dtype) for value in results] + [dma((5, 2)), dma((5, 2))],
        compiler_params=pltpu.CompilerParams(vmem_limit_bytes=62 * 2**20),
    )(*results)
    return tuple(value[None] for value in results)


def solution(mesh):
    rows_spec = P("section", ("rep", "exp"), None)
    weight_spec = P("section", "exp", "rep", None)
    return jax.shard_map(
        shards,
        mesh=mesh,
        in_specs=(rows_spec,) * 5 + (weight_spec,) * 3,
        out_specs=(rows_spec,) * 2 + (weight_spec,) * 3,
        check_vma=False,
    )
```
